256 devices in a mesh: section: 8 (over z), expert: 32 (over y, x, core).
Axes of the slice: x: 4, y: 4, z: 8, core: 2. Of those that a mesh axis runs over, the one named last changes fastest.
Arguments:
- x_saved: bfloat16 [8, 8, 512, 2560], P('section', None, 'expert'), may hold values from -6 to 6
- routes: int32 [8, 8, 512, 2], P('section', None, 'expert'), may hold values from 0 to 15, all different within a row; in each aligned block of 16 rows (0 to 15, 16 to 31, ..., all dimensions but the last counted through in order) at most 3 rows name the same one
- gates: float32 [8, 8, 512, 2], P('section', None, 'expert'), may hold values from 0.1 to 0.6
- cotangent: bfloat16 [8, 512, 2560], P(None, 'expert', 'section'), may hold values from -6 to 6
- w_gate: bfloat16 [8, 12288, 2560], P('section', 'expert'), may hold values from -0.125 to 0.125
- w_up: bfloat16 [8, 12288, 2560], P('section', 'expert'), may hold values from -0.125 to 0.125
- w_down: bfloat16 [8, 12288, 2560], P('section', 'expert'), may hold values from -0.21875 to 0.21875
Outputs:
- grad_inputs: bfloat16 [8, 8, 512, 2560], P('section', None, 'expert')
- grad_gate: bfloat16 [8, 12288, 2560], P('section', 'expert')
- grad_up: bfloat16 [8, 12288, 2560], P('section', 'expert')
- grad_down: bfloat16 [8, 12288, 2560], P('section', 'expert')
The draws below stay inside these ranges and needn't reach their ends.
Inputs may be any that keep to these rules, and one draw needn't show every extreme that they name: `routes`: each token names 2 different experts. In each aligned block of 16 tokens (one device's tokens of one section and micro-batch), no expert is named by more than 3 tokens, and in some blocks one is named by exactly 3.
All inputs are finite; a program needn't handle non-finite values.
Results may differ from the reference program's by a relative error of at most 0.025.
Values may be sent and summed in bfloat16 or wider, within the bound.
No kernel may reach another device: no remote copies, remote signals or barrier semaphores. Data moves between devices by JAX's collectives and lax.ppermute only.
A program may use at most 128 MiB of HBM per device.

```python
import math
import jax
import jax.numpy as jnp
import numpy as np
from jax import lax

D = 2560
FF = 768
SPLIT = 2
TOP = 2
MB = 8
TOK_DEV = 16
SECTIONS = 8
EXP_SECTION = 16
FF_DEV = 384
CAP = 3
TOKENS = 512
N_EXPERT = 32


def steps_of(stream_key, shape, shards, smallest, top_value):
    factor_of = 1.0
    for dim, shards_of in shards:
        steps = jax.random.uniform(jax.random.fold_in(jax.random.fold_in(stream_key, 6), dim), (shards_of,), jnp.float32, smallest / len(shards), top_value / len(shards))
        factor_of = factor_of * jnp.repeat(jnp.exp(steps), shape[dim] // shards_of).reshape((-1,) + (1,) * (len(shape) - 1 - dim))
    return factor_of


def shared_out(own_key, own, number, rows, number_of, top, most, lean):
    sequence = jax.random.permutation(own_key, number_of)
    heavy_load, usual = load_shares(number_of, rows * top, most, lean, True), load_shares(number_of, rows * top, most, lean, False)
    places = jnp.arange(number_of)

    def named(lengths, offset_by):
        used = int((lengths > 0).sum())
        fixed = max(1, used // 4)
        passed = fixed + (places - fixed + offset_by * (used - fixed)) % max(1, number_of - fixed)
        return jnp.zeros((number_of,), jnp.int32).at[sequence[jnp.where(places < fixed, places, passed)]].set(jnp.asarray(lengths, jnp.int32))

    lengths = jnp.where(number % 4 == 0, named(heavy_load, number // 4), named(usual, number - number // 4 - 1))
    mixed = jax.random.permutation(jax.random.fold_in(own, 3), number_of)
    donor, taker = mixed[0:number_of // 2 * 2:2], mixed[1:number_of // 2 * 2:2]
    margin = jnp.minimum(lengths[donor] - 1, most - lengths[taker]) // 2
    margin = jnp.where((donor == sequence[0]) | (taker == sequence[0]) | (lengths[taker] == 0), 0, jnp.maximum(margin, 0))
    passed = jax.random.randint(jax.random.fold_in(own, 4), (number_of // 2,), 0, 1 << 20) % (margin + 1)
    lengths = lengths.at[donor].add(-passed).at[taker].add(passed)
    members = jnp.searchsorted(jnp.cumsum(lengths), jnp.arange(rows * top), side="right").astype(jnp.int32)
    table = members.reshape(top, rows).T
    table = table[jax.random.permutation(jax.random.fold_in(own, 1), rows)]
    offset_by = jax.random.randint(jax.random.fold_in(own, 2), (rows, 1), 0, top)
    return jnp.take_along_axis(table, (jnp.arange(top)[None, :] + offset_by) % top, axis=1)


def load_shares(amount, total, bound, lean, full):
    weights = [(1 << 20) // math.isqrt(standing ** lean) + 1 for standing in range(1, amount + 1)]
    largest = bound if full else min(bound, max(-(-total // amount), total * weights[0] // sum(weights)))
    least = 1 if total - largest >= amount - 1 else 0
    given, surplus = [largest] + [least] * (amount - 1), total - largest - least * (amount - 1)
    while surplus > 0:
        candidates = [i for i in range(1, amount) if given[i] < largest] or [i for i in range(1, amount) if given[i] < bound]
        pool, left = sum([weights[i] for i in candidates]), surplus
        for i in candidates:
            extra = min(bound - given[i], max(1, left * weights[i] // pool), surplus)
            given[i] = given[i] + extra
            surplus = surplus - extra
    return np.array(given)


def gaussian(key, dims, scale, bound, shards=(), held_as=jnp.bfloat16):
    loudness = steps_of(key, dims, shards, -0.22, 0.18) if shards else 1.0
    values = jax.random.normal(key, dims, jnp.float32) * scale * loudness
    return jnp.minimum(jnp.maximum(values, -bound), bound).astype(held_as)


def setup_inputs(seed: int = 0) -> dict:
    key_list = jax.random.split(jax.random.key(seed), 8)
    x_saved = gaussian(key_list[0], (SECTIONS, MB, TOKENS, D), 1.0, 6.0, ((0, 8), (2, 32)))
    routes_keys = jax.random.split(jax.random.fold_in(key_list[1], 1), SECTIONS * MB * TOKENS // TOK_DEV)
    routes_turns = jax.random.permutation(jax.random.fold_in(key_list[1], 3), SECTIONS * MB * TOKENS // TOK_DEV)
    routes = jax.vmap(lambda own, number: shared_out(jax.random.fold_in(key_list[1], 2), own, number, TOK_DEV, EXP_SECTION, TOP, CAP, 2))(routes_keys, routes_turns).reshape((SECTIONS, MB, TOKENS, TOP))
    gates = jnp.clip(0.1 + 0.5 * jax.random.uniform(key_list[2], (SECTIONS, MB, TOKENS, TOP), jnp.float32) ** steps_of(key_list[2], (SECTIONS, MB, TOKENS, TOP), ((0, 8), (2, 32)), -0.2, 0.2), 0.1, 0.6)
    cotangent = gaussian(key_list[3], (MB, TOKENS, D), 1.0, 6.0, ((1, 32), (2, 8)))
    w_gate = gaussian(key_list[4], (SECTIONS, EXP_SECTION * FF, D), D ** -0.5, 0.125, ((0, 8), (1, 32)))
    w_up = gaussian(key_list[5], (SECTIONS, EXP_SECTION * FF, D), D ** -0.5, 0.125, ((0, 8), (1, 32)))
    w_down = gaussian(key_list[6], (SECTIONS, EXP_SECTION * FF, D), FF ** -0.5, 0.21875, ((0, 8), (1, 32)))
    return {"x_saved": x_saved, "routes": routes, "gates": gates, "cotangent": cotangent, "w_gate": w_gate, "w_up": w_up, "w_down": w_down}


def swish_parts(pre_gate):
    sigmoid = jax.nn.sigmoid(pre_gate)
    return pre_gate * sigmoid, sigmoid * (1.0 + pre_gate * (1.0 - sigmoid))


def expert_rows(operands):
    rows_in, rows_grad, gate_block, up_block, down_block = operands
    row_count = rows_in.shape[0]
    pre_gate = jnp.dot(rows_in, gate_block.T, preferred_element_type=jnp.float32)
    pre_up = jnp.dot(rows_in, up_block.T, preferred_element_type=jnp.float32)
    swished, slope_act = swish_parts(pre_gate)
    hidden_act = (swished * pre_up).astype(jnp.bfloat16)
    d_hidden = jnp.dot(rows_grad, down_block.T, preferred_element_type=jnp.float32)
    d_gate = (d_hidden * pre_up * slope_act).astype(jnp.bfloat16)
    d_up = (d_hidden * swished).astype(jnp.bfloat16)
    sliced_gate = d_gate.reshape(row_count, SPLIT, FF_DEV).astype(jnp.float32)
    sliced_up = d_up.reshape(row_count, SPLIT, FF_DEV).astype(jnp.float32)
    gate_parts = gate_block.reshape(SPLIT, FF_DEV, D).astype(jnp.float32)
    up_parts = up_block.reshape(SPLIT, FF_DEV, D).astype(jnp.float32)
    slice_part = jnp.einsum("rsf,sfd->srd", sliced_gate, gate_parts, precision=lax.Precision.HIGHEST)
    slice_part = slice_part + jnp.einsum("rsf,sfd->srd", sliced_up, up_parts, precision=lax.Precision.HIGHEST)
    rounded = lax.optimization_barrier(slice_part.astype(jnp.bfloat16))
    row_grad = jnp.sum(rounded.astype(jnp.float32), axis=0)
    gate_sum = jnp.dot(d_gate.T, rows_in, preferred_element_type=jnp.float32)
    up_sum = jnp.dot(d_up.T, rows_in, preferred_element_type=jnp.float32)
    down_sum = jnp.dot(hidden_act.T, rows_grad, preferred_element_type=jnp.float32)
    return row_grad, gate_sum, up_sum, down_sum


def section_batch(input_rows, route_rows, gate_values, upstream, gate_w, up_w, down_w):
    route_blocks = route_rows.reshape(N_EXPERT, TOK_DEV * TOP).astype(jnp.int32)
    route_hot = (route_blocks[:, :, None] == jnp.arange(EXP_SECTION, dtype=jnp.int32)[None, None, :]).astype(jnp.int32)
    earlier = jnp.cumsum(route_hot, axis=1) - route_hot
    position = jnp.sum(earlier * route_hot, axis=2)
    block_index = jnp.arange(N_EXPERT, dtype=jnp.int32)[:, None]
    target = (route_blocks * (N_EXPERT * CAP) + block_index * CAP + position).reshape(-1).astype(jnp.int32)
    slot_total = EXP_SECTION * N_EXPERT * CAP
    input_repeat = jnp.repeat(input_rows, TOP, axis=0)
    scaled = (jnp.repeat(upstream, TOP, axis=0).astype(jnp.float32) * gate_values.reshape(-1, 1)).astype(jnp.bfloat16)
    input_slots = jnp.zeros((slot_total, D), jnp.bfloat16).at[target].set(input_repeat)
    grad_slots = jnp.zeros((slot_total, D), jnp.bfloat16).at[target].set(scaled)
    operands = (input_slots.reshape(EXP_SECTION, N_EXPERT * CAP, D),
                grad_slots.reshape(EXP_SECTION, N_EXPERT * CAP, D),
                gate_w.reshape(EXP_SECTION, FF, D),
                up_w.reshape(EXP_SECTION, FF, D),
                down_w.reshape(EXP_SECTION, FF, D))
    row_grad, gate_sum, up_sum, down_sum = lax.map(expert_rows, operands)
    picked = row_grad.reshape(slot_total, D)[target]
    outgoing = (upstream.astype(jnp.float32) + jnp.sum(picked.reshape(TOKENS, TOP, D), axis=1)).astype(jnp.bfloat16)
    return outgoing, (gate_sum.reshape(EXP_SECTION * FF, D), up_sum.reshape(EXP_SECTION * FF, D), down_sum.reshape(EXP_SECTION * FF, D))


def reference(x_saved, routes, gates, cotangent, w_gate, w_up, w_down):
    def one_section(upstream_all, section_inputs):
        input_section, route_section, gate_section, gate_w, up_w, down_w = section_inputs

        def one_batch(running, batch_inputs):
            input_rows, route_rows, gate_values, upstream = batch_inputs
            outgoing, batch_sums = section_batch(input_rows, route_rows, gate_values, upstream, gate_w, up_w, down_w)
            return tuple(earlier_sum + batch_sum for earlier_sum, batch_sum in zip(running, batch_sums)), outgoing

        zero_grad = jnp.zeros((EXP_SECTION * FF, D), jnp.float32)
        running, outgoing_all = lax.scan(one_batch, (zero_grad, zero_grad, zero_grad), (input_section, route_section, gate_section, upstream_all))
        grads = tuple((running_sum / MB).astype(jnp.bfloat16) for running_sum in running)
        return outgoing_all, (outgoing_all,) + grads

    unused, stacked = lax.scan(one_section, cotangent, (x_saved, routes, gates, w_gate, w_up, w_down), reverse=True)
    return stacked[0], stacked[1], stacked[2], stacked[3]
```

```python
import jax
import jax.numpy as jnp
from jax import lax
from jax.sharding import PartitionSpec as P

SPLIT = 2
GROUP = 2
ROOM = 4

ROWS_ROWS = (((0,), (0,)), ((), ()))
COLS_COLS = (((1,), (1,)), ((), ()))


def dot(left, right, dims=(((1,), (0,)), ((), ()))):
    return lax.dot_general(left, right, dims, preferred_element_type=jnp.float32)


def slot_tables(routes, gates, experts):
    batches, tokens, top = routes.shape
    groups = batches // GROUP
    rows = tokens * top
    flat = routes.reshape(batches, rows)
    same = flat[:, :, None] == flat[:, None, :]
    before = jnp.arange(rows)[:, None] > jnp.arange(rows)[None, :]
    position = jnp.sum(jnp.logical_and(same, before[None]).astype(jnp.int32), axis=2)
    half = jnp.arange(batches, dtype=jnp.int32)[:, None] % GROUP
    slot = flat * (GROUP * ROOM) + half * ROOM + position
    slot = slot.reshape(groups, 1, GROUP * tokens, top)
    slots = jnp.arange(experts * GROUP * ROOM, dtype=jnp.int32)[None, :, None, None]
    hit = slots == slot
    gate = jnp.where(hit, gates.reshape(groups, 1, GROUP * tokens, top), 0.0)
    placing = jnp.any(hit, axis=3).astype(jnp.bfloat16)
    return placing, jnp.sum(gate, axis=(2, 3))


def on_device(x_saved, routes, gates, cotangent, w_gate, w_up, w_down):
    sections = lax.axis_size("section")
    devices_wide = lax.axis_size("expert")
    section_index = lax.axis_index("section")
    chips = devices_wide // SPLIT
    _, batches, tokens, width = x_saved.shape
    groups = batches // GROUP
    block = GROUP * ROOM
    rows = chips * block
    hidden = w_gate.shape[1]
    same_core = [[SPLIT * c + k for c in range(chips)] for k in range(SPLIT)]
    swap = [(i, i ^ 1) for i in range(devices_wide)]
    ring = [(i, (i - 1) % sections) for i in range(sections)]

    def across(value):
        shaped = value.reshape(chips, -1, width)
        out = lax.all_to_all(shaped, "expert", 0, 0, axis_index_groups=same_core, tiled=True)
        return out.reshape(value.shape)

    def swapped(value):
        return lax.ppermute(value, "expert", swap)

    gate_rows, up_rows, down_rows = w_gate[0], w_up[0], w_down[0]
    both_rows = jnp.concatenate([gate_rows, up_rows], axis=0)

    by_group = cotangent.reshape(groups, GROUP * tokens, -1)
    order = [(z + 1) % sections if (z + 1) % sections < groups else 0 for z in range(sections)]
    pieces = jnp.stack([by_group[g] for g in order])
    pieces = lax.all_to_all(pieces, "section", 0, 0, tiled=True)
    arriving = pieces.transpose(1, 0, 2).reshape(GROUP * tokens, width)

    placing, slot_gates = slot_tables(routes[0], gates[0], chips)
    placing = jnp.concatenate([placing, jnp.zeros_like(placing[:1])])
    slot_gates = jnp.concatenate([slot_gates, jnp.zeros_like(slot_gates[:1])])

    x_groups = x_saved[0].reshape(groups, GROUP * tokens, width)
    x_slots = jnp.einsum(
        "gst,gtd->gsd", placing[:groups], x_groups, preferred_element_type=jnp.float32
    ).astype(jnp.bfloat16)
    x_slots = x_slots.reshape(groups, chips, block, width).transpose(1, 0, 2, 3)
    x_mine = across(x_slots.reshape(chips * groups * block, width))
    x_mine = x_mine.reshape(chips, groups, block, width).transpose(1, 0, 2, 3)
    x_mine = x_mine.reshape(groups, rows, width)
    x_all = jnp.concatenate([x_mine, swapped(x_mine)], axis=1)
    pre = dot(x_all.reshape(groups * SPLIT * rows, width), both_rows, COLS_COLS)
    pre_gate, pre_up = pre[:, :hidden], pre[:, hidden:]
    sigmoid = jax.nn.sigmoid(pre_gate)
    swished = pre_gate * sigmoid
    hidden_act = (swished * pre_up).astype(jnp.bfloat16)
    gate_slope = pre_up * (sigmoid * (1.0 + pre_gate * (1.0 - sigmoid)))
    slopes = jnp.concatenate([gate_slope, swished], axis=1).reshape(
        groups, SPLIT, rows, 2 * hidden
    )

    results = jnp.zeros((groups + 1, GROUP * tokens, width), jnp.bfloat16)
    kept_rows = jnp.zeros((groups + 1, SPLIT, rows, width), jnp.bfloat16)
    kept_d = jnp.zeros((groups + 1, SPLIT, rows, 2 * hidden), jnp.bfloat16)

    for tick in range(sections + groups - 1):
        group = tick - (sections - 1 - section_index)
        active = jnp.logical_and(group >= 0, group < groups)
        kept = jnp.where(active, group, groups)
        chosen = jnp.clip(group, 0, groups - 1)
        place = placing[kept]
        gate = slot_gates[kept]
        slope = slopes[chosen]

        def hidden_part(rows_grad, slope):
            d_hidden = dot(rows_grad, down_rows, COLS_COLS)
            return (jnp.concatenate([d_hidden, d_hidden], axis=1) * slope).astype(jnp.bfloat16)

        rows_mine = (dot(place, arriving) * gate[:, None]).astype(jnp.bfloat16)
        rows_mine = across(rows_mine)
        rows_other = swapped(rows_mine)
        d_mine = hidden_part(rows_mine, slope[0])
        d_other = hidden_part(rows_other, slope[1])
        part_other = dot(d_other, both_rows).astype(jnp.bfloat16)
        from_other = swapped(part_other)
        part_mine = dot(d_mine, both_rows).astype(jnp.bfloat16)
        summed = part_mine.astype(jnp.float32) + from_other.astype(jnp.float32)
        returned = across(summed.astype(jnp.bfloat16))
        outgoing = (arriving.astype(jnp.float32) + dot(place, returned, ROWS_ROWS)).astype(
            jnp.bfloat16
        )
        arriving = lax.ppermute(outgoing, "section", ring)
        results = lax.dynamic_update_index_in_dim(results, outgoing, kept, 0)
        kept_rows = lax.dynamic_update_slice(kept_rows, rows_mine[None, None], (kept, 0, 0, 0))
        kept_rows = lax.dynamic_update_slice(kept_rows, rows_other[None, None], (kept, 1, 0, 0))
        kept_d = lax.dynamic_update_slice(kept_d, d_mine[None, None], (kept, 0, 0, 0))
        kept_d = lax.dynamic_update_slice(kept_d, d_other[None, None], (kept, 1, 0, 0))

    all_d = kept_d[:groups].reshape(groups * SPLIT * rows, 2 * hidden)
    all_rows = kept_rows[:groups].reshape(groups * SPLIT * rows, width)
    both_grads = (dot(all_d, x_all.reshape(all_rows.shape), ROWS_ROWS) / batches).astype(
        jnp.bfloat16
    )
    grad_down = (dot(hidden_act, all_rows, ROWS_ROWS) / batches).astype(jnp.bfloat16)
    grad_inputs = results[:groups].reshape(1, batches, tokens, width)
    return (grad_inputs, both_grads[None, :hidden], both_grads[None, hidden:], grad_down[None])


def solution(mesh):
    in_specs = (
        P("section", None, "expert", None),
        P("section", None, "expert", None),
        P("section", None, "expert", None),
        P(None, "expert", "section"),
        P("section", "expert", None),
        P("section", "expert", None),
        P("section", "expert", None),
    )
    out_specs = (
        P("section", None, "expert", None),
        P("section", "expert", None),
        P("section", "expert", None),
        P("section", "expert", None),
    )
    return jax.shard_map(
        on_device, mesh=mesh, in_specs=in_specs, out_specs=out_specs, check_vma=False
    )
```

```python
import jax
import jax.numpy as jnp
from jax import lax
from jax.sharding import PartitionSpec as P

SPLIT = 2
GROUP = 2
ROOM = 4
CAP = 3

ROWS_ROWS = (((0,), (0,)), ((), ()))
COLS_COLS = (((1,), (1,)), ((), ()))


def dot(left, right, dims=(((1,), (0,)), ((), ()))):
    return lax.dot_general(left, right, dims, preferred_element_type=jnp.float32)


def slot_tables(routes, gates, experts):
    batches, tokens, top = routes.shape
    groups = batches // GROUP
    rows = tokens * top
    flat = routes.reshape(batches, rows)
    same = flat[:, :, None] == flat[:, None, :]
    before = jnp.arange(rows)[:, None] > jnp.arange(rows)[None, :]
    position = jnp.sum(jnp.logical_and(same, before[None]).astype(jnp.int32), axis=2)
    batch = jnp.arange(batches, dtype=jnp.int32)[:, None]
    slot = flat * (GROUP * ROOM) + batch % GROUP * ROOM + position
    slot = slot.reshape(groups, 1, GROUP * tokens, top)
    slots = jnp.arange(experts * GROUP * ROOM, dtype=jnp.int32)
    hit = slots[None, :, None, None] == slot
    gate = jnp.where(hit, gates.reshape(groups, 1, GROUP * tokens, top), 0.0)
    placing = jnp.any(hit, axis=3).astype(jnp.bfloat16)
    pack = (flat * batches + batch) * CAP + position
    packs = jnp.arange(experts * batches * CAP, dtype=jnp.int32)
    packing = packs[:, None, None] == pack.reshape(1, batches * tokens, top)
    packing = jnp.any(packing, axis=2).astype(jnp.bfloat16)
    half, place = slots % (GROUP * ROOM) // ROOM, slots % ROOM
    source = slots // (GROUP * ROOM) * batches + half
    source = source + jnp.arange(groups, dtype=jnp.int32)[:, None] * GROUP
    source = jnp.where(place < CAP, source * CAP + place, -1)
    unpacking = (source[:, :, None] == packs[None, None, :]).astype(jnp.bfloat16)
    return placing, jnp.sum(gate, axis=(2, 3)), packing, unpacking


def on_device(x_saved, routes, gates, cotangent, w_gate, w_up, w_down):
    sections = lax.axis_size("section")
    devices_wide = lax.axis_size("expert")
    section_index = lax.axis_index("section")
    chips = devices_wide // SPLIT
    _, batches, tokens, width = x_saved.shape
    groups = batches // GROUP
    block = GROUP * ROOM
    rows = chips * block
    hidden = w_gate.shape[1]
    same_core = [[SPLIT * c + k for c in range(chips)] for k in range(SPLIT)]
    swap = [(i, i ^ 1) for i in range(devices_wide)]
    ring = [(i, (i - 1) % sections) for i in range(sections)]

    def across(value):
        shaped = value.reshape(chips, -1, width)
        out = lax.all_to_all(shaped, "expert", 0, 0, axis_index_groups=same_core, tiled=True)
        return out.reshape(value.shape)

    def swapped(value):
        return lax.ppermute(value, "expert", swap)

    gate_rows, up_rows, down_rows = w_gate[0], w_up[0], w_down[0]
    both_rows = jnp.concatenate([gate_rows, up_rows], axis=0)

    by_group = cotangent.reshape(groups, GROUP * tokens, -1)
    pieces = jnp.concatenate([by_group[1:], by_group[: sections - groups], by_group[:1]])
    placing, slot_gates, packing, unpacking = slot_tables(routes[0], gates[0], chips)
    padded_placing = jnp.concatenate([placing, jnp.zeros_like(placing[:1])])
    padded_gates = jnp.concatenate([slot_gates, jnp.zeros_like(slot_gates[:1])])
    pieces = lax.all_to_all(pieces, "section", 0, 0, tiled=True)

    x_tokens = x_saved[0].reshape(batches * tokens, width)
    packed = packing.shape[0] // chips
    first = section_index == sections - 1
    start_place = jnp.where(first, placing[0], 0).reshape(chips, block, GROUP * tokens)
    start_place = jnp.pad(start_place, ((0, 0), (0, packed), (0, 0)))
    start_pack = jnp.pad(packing.reshape(chips, packed, -1), ((0, 0), (block, 0), (0, 0)))
    start_place = jnp.concatenate([start_place, start_pack], axis=2)
    start_place = start_place.reshape(chips * (block + packed), -1)
    start_gate = jnp.pad(
        slot_gates[0].reshape(chips, block), ((0, 0), (0, packed)), constant_values=1.0
    ).reshape(-1, 1)
    pieces, both_rows, padded_placing, padded_gates, start_place, start_gate, unpacking = (
        lax.optimization_barrier(
            (pieces, both_rows, padded_placing, padded_gates, start_place, start_gate, unpacking)
        )
    )
    arriving = pieces.transpose(1, 0, 2).reshape(GROUP * tokens, width)

    def forward(x_mine, x_other):
        x_both = jnp.concatenate([x_mine, x_other], axis=0)
        pre = dot(x_both, both_rows, COLS_COLS)
        pre_gate, pre_up = pre[:, :hidden], pre[:, hidden:]
        sigmoid = jax.nn.sigmoid(pre_gate)
        swished = pre_gate * sigmoid
        gate_slope = pre_up * (sigmoid * (1.0 + pre_gate * (1.0 - sigmoid)))
        slope = jnp.concatenate([gate_slope, swished], axis=1)
        return x_both, slope, (swished * pre_up).astype(jnp.bfloat16)

    def hidden_part(rows_grad, slope):
        d_hidden = dot(rows_grad, down_rows, COLS_COLS)
        return (jnp.concatenate([d_hidden, d_hidden], axis=1) * slope).astype(jnp.bfloat16)

    x_rows, slopes, hidden_acts = [], [], []
    kept_rows, kept_d, kept_out = [], [], []
    stacked_slopes = None
    ticks = sections + groups - 1
    for tick in range(ticks):
        group = tick - (sections - 1 - section_index)
        active = jnp.logical_and(group >= 0, group < groups)
        place = padded_placing[jnp.where(active, group, groups)]
        gate = padded_gates[jnp.where(active, group, groups)]

        if tick == 0:
            rows_out = dot(start_place, jnp.concatenate([arriving, x_tokens])) * start_gate
            came = across(rows_out.astype(jnp.bfloat16))
            came_other = swapped(came)
            spread = (chips, block + packed, width)
            rows_mine, rows_other = [
                value.reshape(spread)[:, :block].reshape(rows, width)
                for value in (came, came_other)
            ]
            packs = [
                value.reshape(spread)[:, block:].reshape(chips * packed, width)
                for value in (came, came_other)
            ]

            def group_inputs(g, packs):
                found = [dot(unpacking[g], value).astype(jnp.bfloat16) for value in packs]
                return forward(*found)

            parts = [group_inputs(0, packs)]
            slope = parts[0][1]
        else:
            slope = lax.dynamic_index_in_dim(
                stacked_slopes, jnp.clip(group, 0, groups - 1), 0, keepdims=False
            )
            arriving, place, gate, slope = lax.optimization_barrier((arriving, place, gate, slope))
            rows_mine = across((dot(place, arriving) * gate[:, None]).astype(jnp.bfloat16))
            rows_other = swapped(rows_mine)
        d_mine = hidden_part(rows_mine, slope[:rows])
        d_mine, rows_other = lax.optimization_barrier((d_mine, rows_other))
        d_other = hidden_part(rows_other, slope[rows:])
        part_other = dot(d_other, both_rows).astype(jnp.bfloat16)
        from_other = swapped(part_other)
        part_mine = dot(d_mine, both_rows).astype(jnp.bfloat16)
        part_mine, from_other = lax.optimization_barrier((part_mine, from_other))
        summed = part_mine.astype(jnp.float32) + from_other.astype(jnp.float32)
        summed = summed.astype(jnp.bfloat16)
        kept_rows.append((rows_mine, rows_other))
        kept_d.append((d_mine, d_other))
        if tick == 0:
            summed, packs = lax.optimization_barrier((summed, packs))
            parts += [group_inputs(g, packs) for g in range(1, groups)]
            x_rows, slopes, hidden_acts = zip(*parts)
            stacked_slopes = jnp.stack(slopes)
        if tick == ticks - 1:
            summed, kept_rows, kept_d = lax.optimization_barrier((summed, kept_rows, kept_d))
        returned = across(summed)
        outgoing = (arriving.astype(jnp.float32) + dot(place, returned, ROWS_ROWS)).astype(
            jnp.bfloat16
        )
        kept_out.append(outgoing)
        if tick < ticks - 1:
            arriving = lax.ppermute(outgoing, "section", ring)

    all_x = jnp.concatenate(x_rows)
    all_act = jnp.concatenate(hidden_acts)

    def weight_grads(start):
        def products():
            span = range(start, start + groups)
            all_rows = jnp.concatenate([value for t in span for value in kept_rows[t]])
            all_d = jnp.concatenate([value for t in span for value in kept_d[t]])
            pairs = ((all_d[:, :hidden], all_x), (all_d[:, hidden:], all_x), (all_act, all_rows))
            return tuple(
                (dot(left, right, ROWS_ROWS) / batches).astype(jnp.bfloat16)
                for left, right in pairs
            )

        return products

    grads = lax.switch(
        section_index, [weight_grads(sections - 1 - s) for s in range(sections)]
    )
    results = lax.dynamic_slice_in_dim(
        jnp.concatenate(kept_out),
        (sections - 1 - section_index) * GROUP * tokens,
        batches * tokens,
        axis=0,
    )
    return (results.reshape(1, batches, tokens, width),) + tuple(g[None] for g in grads)


def solution(mesh):
    in_specs = (
        P("section", None, "expert", None),
        P("section", None, "expert", None),
        P("section", None, "expert", None),
        P(None, "expert", "section"),
        P("section", "expert", None),
        P("section", "expert", None),
        P("section", "expert", None),
    )
    out_specs = (
        P("section", None, "expert", None),
        P("section", "expert", None),
        P("section", "expert", None),
        P("section", "expert", None),
    )
    return jax.shard_map(
        on_device, mesh=mesh, in_specs=in_specs, out_specs=out_specs, check_vma=False
    )
```

```python
from functools import partial

import jax
import jax.numpy as jnp
from jax import lax
from jax.experimental import pallas as pl
from jax.experimental.pallas import tpu as pltpu
from jax.sharding import PartitionSpec as P

SPLIT = 2
GROUP = 2
ROOM = 4
CAP = 3

ROWS_ROWS = (((0,), (0,)), ((), ()))
COLS_COLS = (((1,), (1,)), ((), ()))


def dot(left, right, dims=(((1,), (0,)), ((), ()))):
    return lax.dot_general(left, right, dims, preferred_element_type=jnp.float32)


def slot_tables(routes, gates, experts):
    batches, tokens, top = routes.shape
    groups = batches // GROUP
    rows = tokens * top
    flat = routes.reshape(batches, rows)
    same = flat[:, :, None] == flat[:, None, :]
    before = jnp.arange(rows)[:, None] > jnp.arange(rows)[None, :]
    position = jnp.sum(jnp.logical_and(same, before[None]).astype(jnp.int32), axis=2)
    batch = jnp.arange(batches, dtype=jnp.int32)[:, None]
    slot = flat * (GROUP * ROOM) + batch % GROUP * ROOM + position
    slot = slot.reshape(groups, 1, GROUP * tokens, top)
    slots = jnp.arange(experts * GROUP * ROOM, dtype=jnp.int32)
    hit = slots[None, :, None, None] == slot
    gate = jnp.where(hit, gates.reshape(groups, 1, GROUP * tokens, top), 0.0)
    placing = jnp.any(hit, axis=3).astype(jnp.bfloat16)
    pack = (flat * batches + batch) * CAP + position
    packs = jnp.arange(experts * batches * CAP, dtype=jnp.int32)
    packing = packs[:, None, None] == pack.reshape(1, batches * tokens, top)
    packing = jnp.any(packing, axis=2).astype(jnp.bfloat16)
    half, place = slots % (GROUP * ROOM) // ROOM, slots % ROOM
    source = slots // (GROUP * ROOM) * batches + half
    source = source + jnp.arange(groups, dtype=jnp.int32)[:, None] * GROUP
    source = jnp.where(place < CAP, source * CAP + place, -1)
    unpacking = (source[:, :, None] == packs[None, None, :]).astype(jnp.bfloat16)
    return placing, jnp.sum(gate, axis=(2, 3)), packing, unpacking


def add_kernel(first, final, batches, chosen, *refs):
    d_halves, row_halves, x_halves, act_halves = refs[:2], refs[2:4], refs[4:6], refs[6:8]
    before, after = (None, refs[8:11]) if first else (refs[8:11], refs[11:14])
    hidden = after[0].shape[0]

    def product(lefts, rights):
        left = jnp.concatenate(lefts, axis=0)
        right = jnp.concatenate(rights, axis=0)
        return dot(left, right, ROWS_ROWS)

    both = product([d[...] for d in d_halves], [x[0] for x in x_halves])
    down = product([act[0] for act in act_halves], [value[...] for value in row_halves])
    for i, term in enumerate((both[:hidden], both[hidden:], down)):
        total = term if first else before[i][...] + term
        after[i][...] = (total / batches).astype(jnp.bfloat16) if final else total


def add_weight_grads(chosen, d_halves, row_halves, x_halves, act_halves, sums, final, batches):
    rows, width = row_halves[0].shape
    hidden = act_halves[0].shape[2]
    tile = 512 if width % 512 == 0 else width
    whole = pl.BlockSpec((rows, 2 * hidden), lambda n, at: (0, 0))
    row_tile = pl.BlockSpec((rows, tile), lambda n, at: (0, n))
    x_tile = pl.BlockSpec((1, rows, tile), lambda n, at: (at[0], 0, n))
    act_tile = pl.BlockSpec((1, rows, hidden), lambda n, at: (at[0], 0, 0))
    sum_tile = pl.BlockSpec((hidden, tile), lambda n, at: (0, n))
    first = sums is None
    held = [] if first else list(sums)
    aliases = {} if first or final else {9 + i: i for i in range(3)}
    held_as = jnp.bfloat16 if final else jnp.float32
    flops = 2 * 3 * SPLIT * rows * hidden * width
    return pl.pallas_call(
        partial(add_kernel, first, final, batches),
        grid_spec=pltpu.PrefetchScalarGridSpec(
            num_scalar_prefetch=1,
            grid=(width // tile,),
            in_specs=[whole] * 2 + [row_tile] * 2 + [x_tile] * 2 + [act_tile] * 2
            + [sum_tile] * len(held),
            out_specs=[sum_tile] * 3,
        ),
        out_shape=[jax.ShapeDtypeStruct((hidden, width), held_as)] * 3,
        input_output_aliases=aliases,
        compiler_params=pltpu.CompilerParams(vmem_limit_bytes=24 * 1024 * 1024),
        cost_estimate=pl.CostEstimate(
            flops=flops, bytes_accessed=6 * 4 * hidden * width, transcendentals=0
        ),
    )(jnp.reshape(chosen, (1,)), *d_halves, *row_halves, *x_halves, *act_halves, *held)


def on_device(x_saved, routes, gates, cotangent, w_gate, w_up, w_down):
    sections = lax.axis_size("section")
    devices_wide = lax.axis_size("expert")
    section_index = lax.axis_index("section")
    chips = devices_wide // SPLIT
    _, batches, tokens, width = x_saved.shape
    groups = batches // GROUP
    block = GROUP * ROOM
    rows = chips * block
    hidden = w_gate.shape[1]
    same_core = [[SPLIT * c + k for c in range(chips)] for k in range(SPLIT)]
    swap = [(i, i ^ 1) for i in range(devices_wide)]
    ring = [(i, (i - 1) % sections) for i in range(sections)]

    def across(value):
        shaped = value.reshape(chips, -1, width)
        out = lax.all_to_all(shaped, "expert", 0, 0, axis_index_groups=same_core, tiled=True)
        return out.reshape(value.shape)

    def swapped(value):
        return lax.ppermute(value, "expert", swap)

    gate_rows, up_rows, down_rows = w_gate[0], w_up[0], w_down[0]
    both_rows = jnp.concatenate([gate_rows, up_rows], axis=0)

    placing, slot_gates, packing, unpacking = slot_tables(routes[0], gates[0], chips)
    x_tokens = x_saved[0].reshape(batches * tokens, width)
    x_packed = across(dot(packing, x_tokens).astype(jnp.bfloat16))

    by_group = cotangent.reshape(groups, GROUP * tokens, -1)
    pieces = jnp.concatenate([by_group[1:], by_group[: sections - groups], by_group[:1]])
    padded_placing = jnp.concatenate([placing, jnp.zeros_like(placing[:1])])
    padded_gates = jnp.concatenate([slot_gates, jnp.zeros_like(slot_gates[:1])])
    x_packed, pieces, both_rows, padded_placing, padded_gates, unpacking = (
        lax.optimization_barrier(
            (x_packed, pieces, both_rows, padded_placing, padded_gates, unpacking)
        )
    )
    pieces = lax.all_to_all(pieces, "section", 0, 0, tiled=True)
    arriving = pieces.transpose(1, 0, 2).reshape(GROUP * tokens, width)

    def forward(packed):
        x = dot(unpacking.reshape(groups * rows, -1), packed).astype(jnp.bfloat16)
        pre = dot(x, both_rows, COLS_COLS)
        pre_gate, pre_up = pre[:, :hidden], pre[:, hidden:]
        sigmoid = jax.nn.sigmoid(pre_gate)
        swished = pre_gate * sigmoid
        gate_slope = pre_up * (sigmoid * (1.0 + pre_gate * (1.0 - sigmoid)))
        slope = jnp.concatenate([gate_slope, swished], axis=1)
        act = (swished * pre_up).astype(jnp.bfloat16)
        return [value.reshape(groups, rows, -1) for value in (x, slope, act)]

    halves = [forward(packed) for packed in (x_packed, swapped(x_packed))]
    x_halves, slope_halves, act_halves = zip(*halves)

    def hidden_part(rows_grad, slope):
        d_hidden = dot(rows_grad, down_rows, COLS_COLS)
        return (jnp.concatenate([d_hidden, d_hidden], axis=1) * slope).astype(jnp.bfloat16)

    kept_out, sums = [], None
    ticks = sections + groups - 1
    for tick in range(ticks):
        group = tick - (sections - 1 - section_index)
        active = jnp.logical_and(group >= 0, group < groups)
        place = padded_placing[jnp.where(active, group, groups)]
        gate = padded_gates[jnp.where(active, group, groups)]
        chosen = jnp.clip(group, 0, groups - 1)
        slopes = [
            lax.dynamic_index_in_dim(value, chosen, 0, keepdims=False) for value in slope_halves
        ]
        if tick > 0:
            arriving, place, gate, slopes = lax.optimization_barrier(
                (arriving, place, gate, slopes)
            )
        rows_mine = across((dot(place, arriving) * gate[:, None]).astype(jnp.bfloat16))
        rows_other = swapped(rows_mine)
        d_mine = hidden_part(rows_mine, slopes[0])
        d_mine, rows_other = lax.optimization_barrier((d_mine, rows_other))
        d_other = hidden_part(rows_other, slopes[1])
        part_other = dot(d_other, both_rows).astype(jnp.bfloat16)
        from_other = swapped(part_other)
        part_mine = dot(d_mine, both_rows).astype(jnp.bfloat16)
        part_mine, from_other = lax.optimization_barrier((part_mine, from_other))
        summed = part_mine.astype(jnp.float32) + from_other.astype(jnp.float32)
        summed = summed.astype(jnp.bfloat16)
        if tick == ticks - 1:
            results = lax.dynamic_slice_in_dim(
                jnp.concatenate(kept_out + [arriving]),
                (sections - 1 - section_index) * GROUP * tokens,
                batches * tokens,
                axis=0,
            )
            summed, results = lax.optimization_barrier((summed, results))
        summed, grads, row_halves = lax.optimization_barrier(
            (summed, (d_mine, d_other), (rows_mine, rows_other))
        )
        sums = add_weight_grads(
            chosen, grads, row_halves, x_halves, act_halves, sums, tick == ticks - 1, batches
        )
        returned = across(summed)
        outgoing = (arriving.astype(jnp.float32) + dot(place, returned, ROWS_ROWS)).astype(
            jnp.bfloat16
        )
        if tick < ticks - 1:
            kept_out.append(outgoing)
            arriving = lax.ppermute(outgoing, "section", ring)

    last = results[-GROUP * tokens :]
    last = jnp.where(section_index == 0, outgoing, last)
    results = lax.dynamic_update_slice(results, last, (results.shape[0] - GROUP * tokens, 0))
    return (results.reshape(1, batches, tokens, width),) + tuple(g[None] for g in sums)


def solution(mesh):
    in_specs = (
        P("section", None, "expert", None),
        P("section", None, "expert", None),
        P("section", None, "expert", None),
        P(None, "expert", "section"),
        P("section", "expert", None),
        P("section", "expert", None),
        P("section", "expert", None),
    )
    out_specs = (
        P("section", None, "expert", None),
        P("section", "expert", None),
        P("section", "expert", None),
        P("section", "expert", None),
    )
    return jax.shard_map(
        on_device, mesh=mesh, in_specs=in_specs, out_specs=out_specs, check_vma=False
    )
```

```python
from functools import partial

import jax
import jax.numpy as jnp
from jax import lax
from jax.experimental import pallas as pl
from jax.experimental.pallas import tpu as pltpu
from jax.sharding import PartitionSpec as P

SPLIT = 2
GROUP = 2
ROOM = 4
CAP = 3

ROWS_ROWS = (((0,), (0,)), ((), ()))
COLS_COLS = (((1,), (1,)), ((), ()))


def dot(left, right, dims=(((1,), (0,)), ((), ()))):
    return lax.dot_general(left, right, dims, preferred_element_type=jnp.float32)


def together(*values):
    return lax.optimization_barrier(values)


def slot_tables(routes, gates, experts):
    batches, tokens, top = routes.shape
    groups = batches // GROUP
    rows = tokens * top
    flat = routes.reshape(batches, rows)
    same = flat[:, :, None] == flat[:, None, :]
    before = jnp.arange(rows)[:, None] > jnp.arange(rows)[None, :]
    position = jnp.sum(jnp.logical_and(same, before[None]).astype(jnp.int32), axis=2)
    batch = jnp.arange(batches, dtype=jnp.int32)[:, None]
    slot = flat * (GROUP * ROOM) + batch % GROUP * ROOM + position
    slot = slot.reshape(groups, 1, GROUP * tokens, top)
    slots = jnp.arange(experts * GROUP * ROOM, dtype=jnp.int32)
    hit = slots[None, :, None, None] == slot
    gate = jnp.where(hit, gates.reshape(groups, 1, GROUP * tokens, top), 0.0)
    placing = jnp.any(hit, axis=3).astype(jnp.bfloat16)
    pack = (flat * batches + batch) * CAP + position
    packs = jnp.arange(experts * batches * CAP, dtype=jnp.int32)
    packing = packs[:, None, None] == pack.reshape(1, batches * tokens, top)
    packing = jnp.any(packing, axis=2).astype(jnp.bfloat16)
    half, place = slots % (GROUP * ROOM) // ROOM, slots % ROOM
    source = slots // (GROUP * ROOM) * batches + half
    source = source + jnp.arange(groups, dtype=jnp.int32)[:, None] * GROUP
    source = jnp.where(place < CAP, source * CAP + place, -1)
    unpacking = (source[:, :, None] == packs[None, None, :]).astype(jnp.bfloat16)
    return placing, jnp.sum(gate, axis=(2, 3)), packing, unpacking


def add_kernel(first, final, batches, chosen, *refs):
    d_halves, row_halves, x_halves, act_halves = refs[:2], refs[2:4], refs[4:6], refs[6:8]
    before, after = (None, refs[8:11]) if first else (refs[8:11], refs[11:14])
    hidden = after[0].shape[0]

    def product(lefts, rights):
        left = jnp.concatenate(lefts, axis=0)
        right = jnp.concatenate(rights, axis=0)
        return dot(left, right, ROWS_ROWS)

    both = product([d[...] for d in d_halves], [x[0] for x in x_halves])
    down = product([act[0] for act in act_halves], [value[...] for value in row_halves])
    for i, term in enumerate((both[:hidden], both[hidden:], down)):
        total = term if first else before[i][...] + term
        after[i][...] = (total / batches).astype(jnp.bfloat16) if final else total


def add_weight_grads(chosen, d_halves, row_halves, x_halves, act_halves, sums, final, batches):
    rows, width = row_halves[0].shape
    hidden = act_halves[0].shape[2]
    tile = 512 if width % 512 == 0 else width
    whole = pl.BlockSpec((rows, 2 * hidden), lambda n, at: (0, 0))
    row_tile = pl.BlockSpec((rows, tile), lambda n, at: (0, n))
    x_tile = pl.BlockSpec((1, rows, tile), lambda n, at: (at[0], 0, n))
    act_tile = pl.BlockSpec((1, rows, hidden), lambda n, at: (at[0], 0, 0))
    sum_tile = pl.BlockSpec((hidden, tile), lambda n, at: (0, n))
    first = sums is None
    held = [] if first else list(sums)
    aliases = {} if first or final else {9 + i: i for i in range(3)}
    held_as = jnp.bfloat16 if final else jnp.float32
    flops = 2 * 3 * SPLIT * rows * hidden * width
    return pl.pallas_call(
        partial(add_kernel, first, final, batches),
        grid_spec=pltpu.PrefetchScalarGridSpec(
            num_scalar_prefetch=1,
            grid=(width // tile,),
            in_specs=[whole] * 2 + [row_tile] * 2 + [x_tile] * 2 + [act_tile] * 2
            + [sum_tile] * len(held),
            out_specs=[sum_tile] * 3,
        ),
        out_shape=[jax.ShapeDtypeStruct((hidden, width), held_as)] * 3,
        input_output_aliases=aliases,
        compiler_params=pltpu.CompilerParams(vmem_limit_bytes=24 * 1024 * 1024),
        cost_estimate=pl.CostEstimate(
            flops=flops, bytes_accessed=6 * 4 * hidden * width, transcendentals=0
        ),
    )(jnp.reshape(chosen, (1,)), *d_halves, *row_halves, *x_halves, *act_halves, *held)


def on_device(x_saved, routes, gates, cotangent, w_gate, w_up, w_down):
    sections = lax.axis_size("section")
    devices_wide = lax.axis_size("expert")
    section_index = lax.axis_index("section")
    chips = devices_wide // SPLIT
    _, batches, tokens, width = x_saved.shape
    groups = batches // GROUP
    block = GROUP * ROOM
    rows = chips * block
    hidden = w_gate.shape[1]
    same_core = [[SPLIT * c + k for c in range(chips)] for k in range(SPLIT)]
    swap = [(i, i ^ 1) for i in range(devices_wide)]
    ring = [(i, (i - 1) % sections) for i in range(sections)]

    def across(value):
        shaped = value.reshape(chips, -1, width)
        out = lax.all_to_all(shaped, "expert", 0, 0, axis_index_groups=same_core, tiled=True)
        return out.reshape(value.shape)

    def swapped(value):
        return lax.ppermute(value, "expert", swap)

    gate_rows, up_rows, down_rows = w_gate[0], w_up[0], w_down[0]
    both_rows = jnp.concatenate([gate_rows, up_rows], axis=0)

    placing, slot_gates, packing, unpacking = slot_tables(routes[0], gates[0], chips)
    x_tokens = x_saved[0].reshape(batches * tokens, width)
    x_packed = across(dot(packing, x_tokens).astype(jnp.bfloat16))

    by_group = cotangent.reshape(groups, GROUP * tokens, -1)
    pieces = jnp.concatenate([by_group[1:], by_group[: sections - groups], by_group[:1]])
    padded_placing = jnp.concatenate([placing, jnp.zeros_like(placing[:1])])
    padded_gates = jnp.concatenate([slot_gates, jnp.zeros_like(slot_gates[:1])])
    x_packed, pieces, both_rows, padded_placing, padded_gates, unpacking = together(
        x_packed, pieces, both_rows, padded_placing, padded_gates, unpacking
    )
    x_packed_other = swapped(x_packed)
    pieces = lax.all_to_all(pieces, "section", 0, 0, tiled=True)
    arriving = pieces.transpose(1, 0, 2).reshape(GROUP * tokens, width)

    def unpacked(packed):
        return dot(unpacking.reshape(groups * rows, -1), packed).astype(jnp.bfloat16)

    def forward(x):
        pre = dot(x, both_rows, COLS_COLS)
        pre_gate, pre_up = pre[:, :hidden], pre[:, hidden:]
        sigmoid = jax.nn.sigmoid(pre_gate)
        swished = pre_gate * sigmoid
        gate_slope = pre_up * (sigmoid * (1.0 + pre_gate * (1.0 - sigmoid)))
        slope = jnp.concatenate([gate_slope, swished], axis=1)
        return slope, (swished * pre_up).astype(jnp.bfloat16)

    def hidden_part(rows_grad, slope):
        d_hidden = dot(rows_grad, down_rows, COLS_COLS)
        return (jnp.concatenate([d_hidden, d_hidden], axis=1) * slope).astype(jnp.bfloat16)

    def group_at(tick):
        return tick - (sections - 1 - section_index)

    def chosen_at(tick):
        return jnp.clip(group_at(tick), 0, groups - 1)

    x_mine = unpacked(x_packed)
    arriving, x_mine, x_packed_other = together(arriving, x_mine, x_packed_other)

    kept_out, waiting, sums = [], [], None
    ticks = sections + groups - 1
    for tick in range(ticks):
        group = group_at(tick)
        active = jnp.logical_and(group >= 0, group < groups)
        place = padded_placing[jnp.where(active, group, groups)]
        gate = padded_gates[jnp.where(active, group, groups)]
        chosen = chosen_at(tick)
        arriving, place, gate = together(arriving, place, gate)
        rows_out = (dot(place, arriving) * gate[:, None]).astype(jnp.bfloat16)

        if tick == 0:
            rows_out, x_mine, x_packed_other = together(rows_out, x_mine, x_packed_other)
            came = across(rows_out)
            x_other = unpacked(x_packed_other)
            slopes = [forward(value[:rows])[0] for value in (x_mine, x_other)]
            came, slopes, x_mine, x_other = together(came, slopes, x_mine, x_other)
        else:
            rows_out, waiting, chosen = together(rows_out, waiting, chosen)
            came = across(rows_out)
            slopes = [
                lax.dynamic_index_in_dim(value, chosen, 0, keepdims=False)
                for value in slope_halves
            ]
            if tick > 1:
                for held in waiting:
                    sums = add_weight_grads(*held, x_halves, act_halves, sums, False, batches)
                waiting = []
                came, slopes, sums = together(came, slopes, sums)
            else:
                came, slopes = together(came, slopes)

        rows_mine = came
        rows_other = swapped(rows_mine)
        d_mine = hidden_part(rows_mine, slopes[0])
        d_mine, rows_other = together(d_mine, rows_other)
        d_other = hidden_part(rows_other, slopes[1])
        part_other = dot(d_other, both_rows).astype(jnp.bfloat16)
        from_other = swapped(part_other)
        part_mine = dot(d_mine, both_rows).astype(jnp.bfloat16)
        part_mine, from_other = together(part_mine, from_other)
        summed = part_mine.astype(jnp.float32) + from_other.astype(jnp.float32)
        summed = summed.astype(jnp.bfloat16)
        waiting.append((chosen, (d_mine, d_other), (rows_mine, rows_other)))
        if tick == 0:
            summed, x_mine, x_other = together(summed, x_mine, x_other)
            slope_halves, act_halves = zip(*(forward(value) for value in (x_mine, x_other)))
            slope_halves, act_halves, x_halves = [
                [value.reshape(groups, rows, -1) for value in values]
                for values in (slope_halves, act_halves, (x_mine, x_other))
            ]
        if tick == ticks - 1:
            summed, waiting, kept_out = together(summed, waiting, kept_out)
            results = lax.dynamic_slice_in_dim(
                jnp.concatenate(kept_out + [arriving]),
                (sections - 1 - section_index) * GROUP * tokens,
                batches * tokens,
                axis=0,
            )
        returned = across(summed)
        if tick == ticks - 1:
            sums = add_weight_grads(*waiting[0], x_halves, act_halves, sums, True, batches)
            returned, sums, results = together(returned, sums, results)
        outgoing = (arriving.astype(jnp.float32) + dot(place, returned, ROWS_ROWS)).astype(
            jnp.bfloat16
        )
        if tick < ticks - 1:
            kept_out.append(outgoing)
            arriving = lax.ppermute(outgoing, "section", ring)
        if tick == 0:
            arriving, slope_halves, act_halves, x_halves = together(
                arriving, slope_halves, act_halves, x_halves
            )

    last = results[-GROUP * tokens :]
    last = jnp.where(section_index == 0, outgoing, last)
    results = lax.dynamic_update_slice(results, last, (results.shape[0] - GROUP * tokens, 0))
    return (results.reshape(1, batches, tokens, width),) + tuple(g[None] for g in sums)


def solution(mesh):
    in_specs = (
        P("section", None, "expert", None),
        P("section", None, "expert", None),
        P("section", None, "expert", None),
        P(None, "expert", "section"),
        P("section", "expert", None),
        P("section", "expert", None),
        P("section", "expert", None),
    )
    out_specs = (
        P("section", None, "expert", None),
        P("section", "expert", None),
        P("section", "expert", None),
        P("section", "expert", None),
    )
    return jax.shard_map(
        on_device, mesh=mesh, in_specs=in_specs, out_specs=out_specs, check_vma=False
    )
```

```python
from functools import partial

import jax
import jax.numpy as jnp
from jax import lax
from jax.experimental import pallas as pl
from jax.experimental.pallas import tpu as pltpu
from jax.sharding import PartitionSpec as P

SPLIT = 2
GROUP = 2
ROOM = 4
CAP = 3
CHUNKS = 2

ROWS_ROWS = (((0,), (0,)), ((), ()))
COLS_COLS = (((1,), (1,)), ((), ()))


def dot(left, right, dims=(((1,), (0,)), ((), ()))):
    return lax.dot_general(left, right, dims, preferred_element_type=jnp.float32)


def together(*values):
    return lax.optimization_barrier(values)


def slot_tables(routes, gates, experts):
    batches, tokens, top = routes.shape
    groups = batches // GROUP
    rows = tokens * top
    flat = routes.reshape(batches, rows)
    same = flat[:, :, None] == flat[:, None, :]
    before = jnp.arange(rows)[:, None] > jnp.arange(rows)[None, :]
    position = jnp.sum(jnp.logical_and(same, before[None]).astype(jnp.int32), axis=2)
    batch = jnp.arange(batches, dtype=jnp.int32)[:, None]
    slot = flat * (GROUP * ROOM) + batch % GROUP * ROOM + position
    slot = slot.reshape(groups, 1, GROUP * tokens, top)
    slots = jnp.arange(experts * GROUP * ROOM, dtype=jnp.int32)
    hit = slots[None, :, None, None] == slot
    gate = jnp.where(hit, gates.reshape(groups, 1, GROUP * tokens, top), 0.0)
    placing = jnp.any(hit, axis=3).astype(jnp.bfloat16)
    pack = (flat * batches + batch) * CAP + position
    packs = jnp.arange(experts * batches * CAP, dtype=jnp.int32)
    packing = packs[:, None, None] == pack.reshape(1, batches * tokens, top)
    packing = jnp.any(packing, axis=2).astype(jnp.bfloat16)
    half, place = slots % (GROUP * ROOM) // ROOM, slots % ROOM
    source = slots // (GROUP * ROOM) * batches + half
    source = source + jnp.arange(groups, dtype=jnp.int32)[:, None] * GROUP
    source = jnp.where(place < CAP, source * CAP + place, -1)
    unpacking = (source[:, :, None] == packs[None, None, :]).astype(jnp.bfloat16)
    return placing, jnp.sum(gate, axis=(2, 3)), packing, unpacking


def grads_kernel(sections, batches, first_ref, *refs):
    groups = refs[-5].shape[0]
    ticks = sections + groups - 1
    kept = [refs[4 * t : 4 * t + 4] for t in range(ticks)]
    x_halves, act_halves = refs[4 * ticks : 4 * ticks + 2], refs[4 * ticks + 2 : 4 * ticks + 4]
    outs = refs[4 * ticks + 4 : 4 * ticks + 7]
    d_buf, act_buf, rows_buf, x_buf, sems = refs[-5:]
    chunk = rows_buf.shape[-1]
    hidden = act_buf.shape[-1]
    step = pl.program_id(0)
    pairs = [(g, h) for g in range(groups) for h in range(SPLIT)]

    def columns(c):
        return pl.ds(c * chunk, chunk)

    def d_copies(first):
        return [
            pltpu.make_async_copy(kept[first + g][h], d_buf.at[g, h], sems.at[g * SPLIT + h])
            for g, h in pairs
        ]

    def act_copies():
        at = len(pairs)
        return [
            pltpu.make_async_copy(act_halves[h], act_buf.at[:, h], sems.at[at + h])
            for h in range(SPLIT)
        ]

    def x_copies(c):
        at = len(pairs) + SPLIT + c * SPLIT
        return [
            pltpu.make_async_copy(
                x_halves[h].at[:, :, columns(c)], x_buf.at[c, :, h], sems.at[at + h]
            )
            for h in range(SPLIT)
        ]

    def row_copies(c, first):
        at = len(pairs) + SPLIT + CHUNKS * SPLIT + c * len(pairs)
        return [
            pltpu.make_async_copy(
                kept[first + g][SPLIT + h].at[:, columns(c)],
                rows_buf.at[c, g, h],
                sems.at[at + g * SPLIT + h],
            )
            for g, h in pairs
        ]

    @pl.when(step == 0)
    def start():
        for copy in x_copies(0) + act_copies():
            copy.start()
        for first in range(sections):

            @pl.when(first_ref[0] == first)
            def start_kept():
                copies = d_copies(first)
                for c in range(CHUNKS):
                    copies = copies + row_copies(c, first)
                for copy in copies:
                    copy.start()

        for c in range(1, CHUNKS):
            for copy in x_copies(c):
                copy.start()
        for copy in d_copies(0) + act_copies():
            copy.wait()

    def merged(value):
        return value.reshape(-1, value.shape[-1])

    for c in range(CHUNKS):

        @pl.when(step == c)
        def compute():
            for copy in x_copies(c) + row_copies(c, 0):
                copy.wait()
            both = dot(merged(d_buf[...]), merged(x_buf[c]), ROWS_ROWS) / batches
            outs[0][...] = both[:hidden].astype(jnp.bfloat16)
            outs[1][...] = both[hidden:].astype(jnp.bfloat16)
            down = dot(merged(act_buf[...]), merged(rows_buf[c]), ROWS_ROWS) / batches
            outs[2][...] = down.astype(jnp.bfloat16)


def weight_grads(first, kept, x_halves, act_halves, sections, batches):
    groups, rows, width = x_halves[0].shape
    hidden = act_halves[0].shape[2]
    chunk = width // CHUNKS
    operands = [value for tick in kept for value in tick] + list(x_halves) + list(act_halves)
    anywhere = pl.BlockSpec(memory_space=pl.ANY)
    copies = (1 + CHUNKS) * (groups + 1) * SPLIT
    halves = (groups, SPLIT, rows)
    work = groups * SPLIT * rows * width
    return pl.pallas_call(
        partial(grads_kernel, sections, batches),
        grid_spec=pltpu.PrefetchScalarGridSpec(
            num_scalar_prefetch=1,
            grid=(CHUNKS,),
            in_specs=[anywhere] * len(operands),
            out_specs=[pl.BlockSpec((hidden, chunk), lambda n, first: (0, n))] * 3,
            scratch_shapes=[
                pltpu.VMEM(halves + (2 * hidden,), jnp.bfloat16),
                pltpu.VMEM(halves + (hidden,), jnp.bfloat16),
                pltpu.VMEM((CHUNKS,) + halves + (chunk,), jnp.bfloat16),
                pltpu.VMEM((CHUNKS,) + halves + (chunk,), jnp.bfloat16),
                pltpu.SemaphoreType.DMA((copies,)),
            ],
        ),
        out_shape=[jax.ShapeDtypeStruct((hidden, width), jnp.bfloat16)] * 3,
        compiler_params=pltpu.CompilerParams(vmem_limit_bytes=56 * 1024 * 1024),
        cost_estimate=pl.CostEstimate(
            flops=6 * work * hidden, bytes_accessed=4 * work + 6 * hidden * width,
            transcendentals=0,
        ),
    )(jnp.reshape(first, (1,)), *operands)


def on_device(x_saved, routes, gates, cotangent, w_gate, w_up, w_down):
    sections = lax.axis_size("section")
    devices_wide = lax.axis_size("expert")
    section_index = lax.axis_index("section")
    chips = devices_wide // SPLIT
    _, batches, tokens, width = x_saved.shape
    groups = batches // GROUP
    block = GROUP * ROOM
    rows = chips * block
    hidden = w_gate.shape[1]
    same_core = [[SPLIT * c + k for c in range(chips)] for k in range(SPLIT)]
    swap = [(i, i ^ 1) for i in range(devices_wide)]
    ring = [(i, (i - 1) % sections) for i in range(sections)]

    def across(value):
        shaped = value.reshape(chips, -1, width)
        out = lax.all_to_all(shaped, "expert", 0, 0, axis_index_groups=same_core, tiled=True)
        return out.reshape(value.shape)

    def swapped(value):
        return lax.ppermute(value, "expert", swap)

    gate_rows, up_rows, down_rows = w_gate[0], w_up[0], w_down[0]
    both_rows = jnp.concatenate([gate_rows, up_rows], axis=0)

    placing, slot_gates, packing, unpacking = slot_tables(routes[0], gates[0], chips)
    x_tokens = x_saved[0].reshape(batches * tokens, width)
    x_packed = across(dot(packing, x_tokens).astype(jnp.bfloat16))

    by_group = cotangent.reshape(groups, GROUP * tokens, -1)
    pieces = jnp.concatenate([by_group[1:], by_group[: sections - groups], by_group[:1]])
    padded_placing = jnp.concatenate([placing, jnp.zeros_like(placing[:1])])
    padded_gates = jnp.concatenate([slot_gates, jnp.zeros_like(slot_gates[:1])])
    x_packed, pieces, both_rows, padded_placing, padded_gates, unpacking = together(
        x_packed, pieces, both_rows, padded_placing, padded_gates, unpacking
    )
    x_packed_other = swapped(x_packed)
    pieces = lax.all_to_all(pieces, "section", 0, 0, tiled=True)
    arriving = pieces.transpose(1, 0, 2).reshape(GROUP * tokens, width)

    def unpacked(packed):
        return dot(unpacking.reshape(groups * rows, -1), packed).astype(jnp.bfloat16)

    def forward(x):
        pre = dot(x, both_rows, COLS_COLS)
        pre_gate, pre_up = pre[:, :hidden], pre[:, hidden:]
        sigmoid = jax.nn.sigmoid(pre_gate)
        swished = pre_gate * sigmoid
        gate_slope = pre_up * (sigmoid * (1.0 + pre_gate * (1.0 - sigmoid)))
        slope = jnp.concatenate([gate_slope, swished], axis=1)
        return slope, (swished * pre_up).astype(jnp.bfloat16)

    def hidden_part(rows_grad, slope):
        d_hidden = dot(rows_grad, down_rows, COLS_COLS)
        return (jnp.concatenate([d_hidden, d_hidden], axis=1) * slope).astype(jnp.bfloat16)

    def group_at(tick):
        return tick - (sections - 1 - section_index)

    def chosen_at(tick):
        return jnp.clip(group_at(tick), 0, groups - 1)

    x_mine = unpacked(x_packed)
    arriving, x_mine, x_packed_other = together(arriving, x_mine, x_packed_other)

    kept_out, kept = [], []
    ticks = sections + groups - 1
    for tick in range(ticks):
        group = group_at(tick)
        active = jnp.logical_and(group >= 0, group < groups)
        place = padded_placing[jnp.where(active, group, groups)]
        gate = padded_gates[jnp.where(active, group, groups)]
        if tick == 0:
            rows_out = (dot(place, arriving) * gate[:, None]).astype(jnp.bfloat16)
            rows_out, x_mine, x_packed_other = together(rows_out, x_mine, x_packed_other)
            came = across(rows_out)
            x_other = unpacked(x_packed_other)
            slopes = [forward(value[:rows])[0] for value in (x_mine, x_other)]
            rows_mine, slopes, x_mine, x_other = together(came, slopes, x_mine, x_other)
        else:
            slopes = [
                lax.dynamic_index_in_dim(value, chosen_at(tick), 0, keepdims=False)
                for value in slope_halves
            ]
            arriving, place, gate, slopes = together(arriving, place, gate, slopes)
            rows_mine = across((dot(place, arriving) * gate[:, None]).astype(jnp.bfloat16))
        rows_other = swapped(rows_mine)
        d_mine = hidden_part(rows_mine, slopes[0])
        d_mine, rows_other = together(d_mine, rows_other)
        d_other = hidden_part(rows_other, slopes[1])
        part_other = dot(d_other, both_rows).astype(jnp.bfloat16)
        from_other = swapped(part_other)
        part_mine = dot(d_mine, both_rows).astype(jnp.bfloat16)
        part_mine, from_other = together(part_mine, from_other)
        summed = part_mine.astype(jnp.float32) + from_other.astype(jnp.float32)
        summed = summed.astype(jnp.bfloat16)
        if tick == 0:
            summed, x_mine, x_other = together(summed, x_mine, x_other)
            slope_halves, act_halves = zip(*(forward(value) for value in (x_mine, x_other)))
            slope_halves, act_halves, x_halves = [
                [value.reshape(groups, rows, -1) for value in values]
                for values in (slope_halves, act_halves, (x_mine, x_other))
            ]
        if tick == ticks - 1:
            first = sections - 1 - section_index
            summed, d_mine, d_other, rows_mine, rows_other, first = together(
                summed, d_mine, d_other, rows_mine, rows_other, first
            )
        kept.append((d_mine, d_other, rows_mine, rows_other))
        returned = across(summed)
        if tick == ticks - 1:
            grads = weight_grads(first, kept, x_halves, act_halves, sections, batches)
            results = lax.dynamic_slice_in_dim(
                jnp.concatenate(kept_out + [arriving]),
                first * (GROUP * tokens),
                batches * tokens,
                axis=0,
            )
            returned, results, grads = together(returned, results, grads)
        outgoing = (arriving.astype(jnp.float32) + dot(place, returned, ROWS_ROWS)).astype(
            jnp.bfloat16
        )
        if tick < ticks - 1:
            kept_out.append(outgoing)
            arriving = lax.ppermute(outgoing, "section", ring)

    last = results[-GROUP * tokens :]
    last = jnp.where(section_index == 0, outgoing, last)
    results = lax.dynamic_update_slice(results, last, (results.shape[0] - GROUP * tokens, 0))
    return (results.reshape(1, batches, tokens, width),) + tuple(g[None] for g in grads)


def solution(mesh):
    in_specs = (
        P("section", None, "expert", None),
        P("section", None, "expert", None),
        P("section", None, "expert", None),
        P(None, "expert", "section"),
        P("section", "expert", None),
        P("section", "expert", None),
        P("section", "expert", None),
    )
    out_specs = (
        P("section", None, "expert", None),
        P("section", "expert", None),
        P("section", "expert", None),
        P("section", "expert", None),
    )
    return jax.shard_map(
        on_device, mesh=mesh, in_specs=in_specs, out_specs=out_specs, check_vma=False
    )
```

```python
from functools import partial

import jax
import jax.numpy as jnp
from jax import lax
from jax.experimental import pallas as pl
from jax.experimental.pallas import tpu as pltpu
from jax.sharding import PartitionSpec as P

SPLIT = 2
GROUP = 2
ROOM = 4
CAP = 3
CHUNKS = 2

ROWS_ROWS = (((0,), (0,)), ((), ()))
COLS_COLS = (((1,), (1,)), ((), ()))


def dot(left, right, dims=(((1,), (0,)), ((), ()))):
    return lax.dot_general(left, right, dims, preferred_element_type=jnp.float32)


def together(*values):
    return lax.optimization_barrier(values)


def slot_tables(routes, gates, experts):
    batches, tokens, top = routes.shape
    groups = batches // GROUP
    rows = tokens * top
    flat = routes.reshape(batches, rows)
    same = flat[:, :, None] == flat[:, None, :]
    before = jnp.arange(rows)[:, None] > jnp.arange(rows)[None, :]
    position = jnp.sum(jnp.logical_and(same, before[None]).astype(jnp.int32), axis=2)
    batch = jnp.arange(batches, dtype=jnp.int32)[:, None]
    slot = flat * (GROUP * ROOM) + batch % GROUP * ROOM + position
    slot = slot.reshape(groups, 1, GROUP * tokens, top)
    slots = jnp.arange(experts * GROUP * ROOM, dtype=jnp.int32)
    hit = slots[None, :, None, None] == slot
    gate = jnp.where(hit, gates.reshape(groups, 1, GROUP * tokens, top), 0.0)
    placing = jnp.any(hit, axis=3).astype(jnp.bfloat16)
    pack = (flat * batches + batch) * CAP + position
    packs = jnp.arange(experts * batches * CAP, dtype=jnp.int32)
    packing = packs[:, None, None] == pack.reshape(1, batches * tokens, top)
    packing = jnp.any(packing, axis=2).astype(jnp.bfloat16)
    half, place = slots % (GROUP * ROOM) // ROOM, slots % ROOM
    source = slots // (GROUP * ROOM) * batches + half
    source = source + jnp.arange(groups, dtype=jnp.int32)[:, None] * GROUP
    source = jnp.where(place < CAP, source * CAP + place, -1)
    unpacking = (source[:, :, None] == packs[None, None, :]).astype(jnp.bfloat16)
    return placing, jnp.sum(gate, axis=(2, 3)), packing, unpacking


def grads_kernel(sections, batches, first_ref, *refs):
    groups = refs[-5].shape[0]
    ticks = sections + groups - 1
    kept = [refs[4 * t : 4 * t + 4] for t in range(ticks)]
    x_halves, act_halves = refs[4 * ticks : 4 * ticks + 2], refs[4 * ticks + 2 : 4 * ticks + 4]
    outs = refs[4 * ticks + 4 : 4 * ticks + 7]
    d_buf, act_buf, rows_buf, x_buf, sems = refs[-5:]
    chunk = rows_buf.shape[-1]
    hidden = act_buf.shape[-1]
    step = pl.program_id(0)
    pairs = [(g, h) for g in range(groups) for h in range(SPLIT)]

    def columns(c):
        return pl.ds(c * chunk, chunk)

    def d_copies(first):
        return [
            pltpu.make_async_copy(kept[first + g][h], d_buf.at[g, h], sems.at[g * SPLIT + h])
            for g, h in pairs
        ]

    def act_copies():
        at = len(pairs)
        return [
            pltpu.make_async_copy(act_halves[h], act_buf.at[:, h], sems.at[at + h])
            for h in range(SPLIT)
        ]

    def x_copies(c):
        at = len(pairs) + SPLIT + c * SPLIT
        return [
            pltpu.make_async_copy(
                x_halves[h].at[:, :, columns(c)], x_buf.at[c, :, h], sems.at[at + h]
            )
            for h in range(SPLIT)
        ]

    def row_copies(c, first):
        at = len(pairs) + SPLIT + CHUNKS * SPLIT + c * len(pairs)
        return [
            pltpu.make_async_copy(
                kept[first + g][SPLIT + h].at[:, columns(c)],
                rows_buf.at[c, g, h],
                sems.at[at + g * SPLIT + h],
            )
            for g, h in pairs
        ]

    @pl.when(step == 0)
    def start():
        for copy in x_copies(0) + act_copies():
            copy.start()
        for first in range(sections):

            @pl.when(first_ref[0] == first)
            def start_kept():
                copies = d_copies(first)
                for c in range(CHUNKS):
                    copies = copies + row_copies(c, first)
                for copy in copies:
                    copy.start()

        for c in range(1, CHUNKS):
            for copy in x_copies(c):
                copy.start()
        for copy in d_copies(0) + act_copies():
            copy.wait()

    def merged(value):
        return value.reshape(-1, value.shape[-1])

    for c in range(CHUNKS):

        @pl.when(step == c)
        def compute():
            for copy in x_copies(c) + row_copies(c, 0):
                copy.wait()
            both = dot(merged(d_buf[...]), merged(x_buf[c]), ROWS_ROWS) / batches
            outs[0][...] = both[:hidden].astype(jnp.bfloat16)
            outs[1][...] = both[hidden:].astype(jnp.bfloat16)
            down = dot(merged(act_buf[...]), merged(rows_buf[c]), ROWS_ROWS) / batches
            outs[2][...] = down.astype(jnp.bfloat16)


def weight_grads(first, kept, x_halves, act_halves, sections, batches):
    groups, rows, width = x_halves[0].shape
    hidden = act_halves[0].shape[2]
    chunk = width // CHUNKS
    operands = [value for tick in kept for value in tick] + list(x_halves) + list(act_halves)
    anywhere = pl.BlockSpec(memory_space=pl.ANY)
    copies = (1 + CHUNKS) * (groups + 1) * SPLIT
    halves = (groups, SPLIT, rows)
    work = groups * SPLIT * rows * width
    return pl.pallas_call(
        partial(grads_kernel, sections, batches),
        grid_spec=pltpu.PrefetchScalarGridSpec(
            num_scalar_prefetch=1,
            grid=(CHUNKS,),
            in_specs=[anywhere] * len(operands),
            out_specs=[pl.BlockSpec((hidden, chunk), lambda n, first: (0, n))] * 3,
            scratch_shapes=[
                pltpu.VMEM(halves + (2 * hidden,), jnp.bfloat16),
                pltpu.VMEM(halves + (hidden,), jnp.bfloat16),
                pltpu.VMEM((CHUNKS,) + halves + (chunk,), jnp.bfloat16),
                pltpu.VMEM((CHUNKS,) + halves + (chunk,), jnp.bfloat16),
                pltpu.SemaphoreType.DMA((copies,)),
            ],
        ),
        out_shape=[jax.ShapeDtypeStruct((hidden, width), jnp.bfloat16)] * 3,
        compiler_params=pltpu.CompilerParams(vmem_limit_bytes=56 * 1024 * 1024),
        cost_estimate=pl.CostEstimate(
            flops=6 * work * hidden, bytes_accessed=4 * work + 6 * hidden * width,
            transcendentals=0,
        ),
    )(jnp.reshape(first, (1,)), *operands)


def on_device(x_saved, routes, gates, cotangent, w_gate, w_up, w_down):
    sections = lax.axis_size("section")
    devices_wide = lax.axis_size("expert")
    section_index = lax.axis_index("section")
    chips = devices_wide // SPLIT
    _, batches, tokens, width = x_saved.shape
    groups = batches // GROUP
    block = GROUP * ROOM
    rows = chips * block
    hidden = w_gate.shape[1]
    same_core = [[SPLIT * c + k for c in range(chips)] for k in range(SPLIT)]
    swap = [(i, i ^ 1) for i in range(devices_wide)]
    ring = [(i, (i - 1) % sections) for i in range(sections)]

    def across(value):
        shaped = value.reshape(chips, -1, width)
        out = lax.all_to_all(shaped, "expert", 0, 0, axis_index_groups=same_core, tiled=True)
        return out.reshape(value.shape)

    def swapped(value):
        return lax.ppermute(value, "expert", swap)

    gate_rows, up_rows, down_rows = w_gate[0], w_up[0], w_down[0]
    both_rows = jnp.concatenate([gate_rows, up_rows], axis=0)

    placing, slot_gates, packing, unpacking = slot_tables(routes[0], gates[0], chips)
    x_tokens = x_saved[0].reshape(batches * tokens, width)
    x_out = dot(packing, x_tokens).astype(jnp.bfloat16)

    by_group = cotangent.reshape(groups, GROUP * tokens, -1)
    blocks = []
    for ahead in range(sections):
        wanted = (section_index + ahead + 1) % sections
        wanted = jnp.where(wanted < groups, wanted, 0)
        blocks.append(lax.dynamic_index_in_dim(by_group, wanted, 0, keepdims=False))
    x_packed = across(x_out)
    step = 1
    while step < sections:
        moved = [k for k in range(sections) if k & step]
        pairs = [(z, (z + step) % sections) for z in range(sections)]
        sent = jnp.concatenate([blocks[k] for k in moved])
        sent = lax.ppermute(sent, "section", pairs).reshape(len(moved), GROUP * tokens, -1)
        for i, k in enumerate(moved):
            blocks[k] = sent[i]
        step *= 2
    arriving = jnp.concatenate(
        [lax.select_n((section_index - j) % sections, *blocks) for j in range(sections)], axis=1
    )
    padded_placing = jnp.concatenate([placing, jnp.zeros_like(placing[:1])])
    padded_gates = jnp.concatenate([slot_gates, jnp.zeros_like(slot_gates[:1])])
    x_packed, arriving, both_rows, padded_placing, padded_gates, unpacking = together(
        x_packed, arriving, both_rows, padded_placing, padded_gates, unpacking
    )
    x_packed_other = swapped(x_packed)

    def unpacked(packed, count):
        place = unpacking[:count].reshape(count * rows, -1)
        return dot(place, packed).astype(jnp.bfloat16)

    def forward(x):
        pre = dot(x, both_rows, COLS_COLS)
        pre_gate, pre_up = pre[:, :hidden], pre[:, hidden:]
        sigmoid = jax.nn.sigmoid(pre_gate)
        swished = pre_gate * sigmoid
        gate_slope = pre_up * (sigmoid * (1.0 + pre_gate * (1.0 - sigmoid)))
        slope = jnp.concatenate([gate_slope, swished], axis=1)
        return slope, (swished * pre_up).astype(jnp.bfloat16)

    def hidden_part(rows_grad, slope):
        d_hidden = dot(rows_grad, down_rows, COLS_COLS)
        return (jnp.concatenate([d_hidden, d_hidden], axis=1) * slope).astype(jnp.bfloat16)

    def group_at(tick):
        return tick - (sections - 1 - section_index)

    def sliced(value, tick):
        chosen = jnp.clip(group_at(tick), 0, groups - 1)
        return lax.dynamic_slice_in_dim(value, chosen * rows, rows, axis=0)

    kept_out, kept = [], []
    ticks = sections + groups - 1
    for tick in range(ticks):
        group = group_at(tick)
        active = jnp.logical_and(group >= 0, group < groups)
        place = padded_placing[jnp.where(active, group, groups)]
        gate = padded_gates[jnp.where(active, group, groups)]
        if tick == 0:
            rows_out = (dot(place, arriving) * gate[:, None]).astype(jnp.bfloat16)
            rows_out, x_packed, x_packed_other = together(rows_out, x_packed, x_packed_other)
            came = across(rows_out)
            x_mine = unpacked(x_packed, groups)
            slopes = [forward(x_mine[:rows])[0], forward(unpacked(x_packed_other, 1))[0]]
            rows_mine, slopes, x_mine = together(came, slopes, x_mine)
        elif tick == 1:
            slope_mine = sliced(slope_mine_all, tick)
            arriving, place, gate, slope_mine, x_other = together(
                arriving, place, gate, slope_mine, x_other
            )
            rows_out = (dot(place, arriving) * gate[:, None]).astype(jnp.bfloat16)
            rows_out, x_other = together(rows_out, x_other)
            came = across(rows_out)
            slope_other_all, act_other = forward(x_other)
            rows_mine, slope_other = together(came, sliced(slope_other_all, tick))
            slopes = [slope_mine, slope_other]
            x_halves, act_halves = [
                [value.reshape(groups, rows, -1) for value in values]
                for values in ((x_mine, x_other), (act_mine, act_other))
            ]
        else:
            slopes = [sliced(slope_mine_all, tick), sliced(slope_other_all, tick)]
            arriving, place, gate, slopes = together(arriving, place, gate, slopes)
            rows_mine = across((dot(place, arriving) * gate[:, None]).astype(jnp.bfloat16))
        rows_other = swapped(rows_mine)
        d_mine = hidden_part(rows_mine, slopes[0])
        d_mine, rows_other = together(d_mine, rows_other)
        d_other = hidden_part(rows_other, slopes[1])
        part_other = dot(d_other, both_rows).astype(jnp.bfloat16)
        from_other = swapped(part_other)
        part_mine = dot(d_mine, both_rows).astype(jnp.bfloat16)
        part_mine, from_other = together(part_mine, from_other)
        summed = part_mine.astype(jnp.float32) + from_other.astype(jnp.float32)
        summed = summed.astype(jnp.bfloat16)
        if tick == 0:
            summed, x_mine, x_packed_other = together(summed, x_mine, x_packed_other)
            slope_mine_all, act_mine = forward(x_mine)
            x_other = unpacked(x_packed_other, groups)
        if tick == ticks - 1:
            first = sections - 1 - section_index
            summed, d_mine, d_other, rows_mine, rows_other, first = together(
                summed, d_mine, d_other, rows_mine, rows_other, first
            )
        kept.append((d_mine, d_other, rows_mine, rows_other))
        returned = across(summed)
        if tick == ticks - 1:
            grads = weight_grads(first, kept, x_halves, act_halves, sections, batches)
            results = lax.dynamic_slice_in_dim(
                jnp.concatenate(kept_out + [arriving]),
                first * (GROUP * tokens),
                batches * tokens,
                axis=0,
            )
            returned, results, grads = together(returned, results, grads)
        outgoing = (arriving.astype(jnp.float32) + dot(place, returned, ROWS_ROWS)).astype(
            jnp.bfloat16
        )
        if tick < ticks - 1:
            kept_out.append(outgoing)
            arriving = lax.ppermute(outgoing, "section", ring)

    last = results[-GROUP * tokens :]
    last = jnp.where(section_index == 0, outgoing, last)
    results = lax.dynamic_update_slice(results, last, (results.shape[0] - GROUP * tokens, 0))
    return (results.reshape(1, batches, tokens, width),) + tuple(g[None] for g in grads)


def solution(mesh):
    in_specs = (
        P("section", None, "expert", None),
        P("section", None, "expert", None),
        P("section", None, "expert", None),
        P(None, "expert", "section"),
        P("section", "expert", None),
        P("section", "expert", None),
        P("section", "expert", None),
    )
    out_specs = (
        P("section", None, "expert", None),
        P("section", "expert", None),
        P("section", "expert", None),
        P("section", "expert", None),
    )
    return jax.shard_map(
        on_device, mesh=mesh, in_specs=in_specs, out_specs=out_specs, check_vma=False
    )
```

```python
from functools import partial

import jax
import jax.numpy as jnp
from jax import lax
from jax.experimental import pallas as pl
from jax.experimental.pallas import tpu as pltpu
from jax.sharding import PartitionSpec as P

SPLIT = 2
GROUP = 2
ROOM = 4
CAP = 3
CHUNKS = 2

ROWS_ROWS = (((0,), (0,)), ((), ()))
COLS_COLS = (((1,), (1,)), ((), ()))


def dot(left, right, dims=(((1,), (0,)), ((), ()))):
    return lax.dot_general(left, right, dims, preferred_element_type=jnp.float32)


def together(*values):
    return lax.optimization_barrier(values)


def slot_tables(routes, gates, experts):
    batches, tokens, top = routes.shape
    groups = batches // GROUP
    rows = tokens * top
    flat = routes.reshape(batches, rows)
    same = flat[:, :, None] == flat[:, None, :]
    before = jnp.arange(rows)[:, None] > jnp.arange(rows)[None, :]
    position = jnp.sum(jnp.logical_and(same, before[None]).astype(jnp.int32), axis=2)
    batch = jnp.arange(batches, dtype=jnp.int32)[:, None]
    slot = flat * (GROUP * ROOM) + batch % GROUP * ROOM + position
    slot = slot.reshape(groups, 1, GROUP * tokens, top)
    slots = jnp.arange(experts * GROUP * ROOM, dtype=jnp.int32)
    hit = slots[None, :, None, None] == slot
    gate = jnp.where(hit, gates.reshape(groups, 1, GROUP * tokens, top), 0.0)
    placing = jnp.any(hit, axis=3).astype(jnp.bfloat16)
    pack = (flat * batches + batch) * CAP + position
    packs = jnp.arange(experts * batches * CAP, dtype=jnp.int32)
    packing = packs[:, None, None] == pack.reshape(1, batches * tokens, top)
    packing = jnp.any(packing, axis=2).astype(jnp.bfloat16)
    half, place = slots % (GROUP * ROOM) // ROOM, slots % ROOM
    source = slots // (GROUP * ROOM) * batches + half
    source = source + jnp.arange(groups, dtype=jnp.int32)[:, None] * GROUP
    source = jnp.where(place < CAP, source * CAP + place, -1)
    unpacking = (source[:, :, None] == packs[None, None, :]).astype(jnp.bfloat16)
    return placing, jnp.sum(gate, axis=(2, 3)), packing, unpacking


def grads_kernel(sections, batches, first_ref, *refs):
    groups = refs[-5].shape[0]
    ticks = sections + groups - 1
    kept = [refs[4 * t : 4 * t + 4] for t in range(ticks)]
    x_halves, act_halves = refs[4 * ticks : 4 * ticks + 2], refs[4 * ticks + 2 : 4 * ticks + 4]
    kept_out, results = refs[4 * ticks + 4 : 5 * ticks + 3], refs[5 * ticks + 3]
    outs = refs[5 * ticks + 4 : 5 * ticks + 7]
    d_buf, act_buf, rows_buf, x_buf, sems = refs[-5:]
    chunk = rows_buf.shape[-1]
    hidden = act_buf.shape[-1]
    step = pl.program_id(0)
    pairs = [(g, h) for g in range(groups) for h in range(SPLIT)]

    def columns(c):
        return pl.ds(c * chunk, chunk)

    def d_copies(first):
        return [
            pltpu.make_async_copy(kept[first + g][h], d_buf.at[g, h], sems.at[g * SPLIT + h])
            for g, h in pairs
        ]

    def act_copies():
        at = len(pairs)
        return [
            pltpu.make_async_copy(act_halves[h], act_buf.at[:, h], sems.at[at + h])
            for h in range(SPLIT)
        ]

    def x_copies(c):
        at = len(pairs) + SPLIT + c * SPLIT
        return [
            pltpu.make_async_copy(
                x_halves[h].at[:, :, columns(c)], x_buf.at[c, :, h], sems.at[at + h]
            )
            for h in range(SPLIT)
        ]

    def row_copies(c, first):
        at = len(pairs) + SPLIT + CHUNKS * SPLIT + c * len(pairs)
        return [
            pltpu.make_async_copy(
                kept[first + g][SPLIT + h].at[:, columns(c)],
                rows_buf.at[c, g, h],
                sems.at[at + g * SPLIT + h],
            )
            for g, h in pairs
        ]

    def result_copies(first):
        at = len(pairs) + SPLIT + CHUNKS * (SPLIT + len(pairs))
        block = kept_out[0].shape[0]
        return [
            pltpu.make_async_copy(
                kept_out[min(first + g, ticks - 2)],
                results.at[pl.ds(g * block, block)],
                sems.at[at + g],
            )
            for g in range(groups)
        ]

    @pl.when(step == 0)
    def start():
        for first in range(sections):

            @pl.when(first_ref[0] == first)
            def start_kept():
                copies = d_copies(first) + x_copies(0) + act_copies() + row_copies(0, first)
                for c in range(1, CHUNKS):
                    copies = copies + x_copies(c) + row_copies(c, first)
                for copy in copies + result_copies(first):
                    copy.start()

        for copy in d_copies(0):
            copy.wait()

    def merged(value):
        return value.reshape(-1, value.shape[-1])

    for c in range(CHUNKS):

        @pl.when(step == c)
        def compute():
            for copy in x_copies(c):
                copy.wait()
            both = dot(merged(d_buf[...]), merged(x_buf[c]), ROWS_ROWS) / batches
            outs[0][...] = both[:hidden].astype(jnp.bfloat16)
            outs[1][...] = both[hidden:].astype(jnp.bfloat16)
            for copy in row_copies(c, 0) + (act_copies() if c == 0 else []):
                copy.wait()
            down = dot(merged(act_buf[...]), merged(rows_buf[c]), ROWS_ROWS) / batches
            outs[2][...] = down.astype(jnp.bfloat16)
            if c == CHUNKS - 1:
                for copy in result_copies(0):
                    copy.wait()


def weight_grads(first, kept, kept_out, x_halves, act_halves, sections, batches):
    groups, rows, width = x_halves[0].shape
    hidden = act_halves[0].shape[2]
    chunk = width // CHUNKS
    operands = [value for tick in kept for value in tick] + list(x_halves) + list(act_halves)
    operands = operands + kept_out
    anywhere = pl.BlockSpec(memory_space=pl.ANY)
    copies = (1 + CHUNKS) * (groups + 1) * SPLIT + groups
    results = jax.ShapeDtypeStruct((groups * kept_out[0].shape[0], width), jnp.bfloat16)
    halves = (groups, SPLIT, rows)
    work = groups * SPLIT * rows * width
    return pl.pallas_call(
        partial(grads_kernel, sections, batches),
        grid_spec=pltpu.PrefetchScalarGridSpec(
            num_scalar_prefetch=1,
            grid=(CHUNKS,),
            in_specs=[anywhere] * len(operands),
            out_specs=[anywhere] + [pl.BlockSpec((hidden, chunk), lambda n, first: (0, n))] * 3,
            scratch_shapes=[
                pltpu.VMEM(halves + (2 * hidden,), jnp.bfloat16),
                pltpu.VMEM(halves + (hidden,), jnp.bfloat16),
                pltpu.VMEM((CHUNKS,) + halves + (chunk,), jnp.bfloat16),
                pltpu.VMEM((CHUNKS,) + halves + (chunk,), jnp.bfloat16),
                pltpu.SemaphoreType.DMA((copies,)),
            ],
        ),
        out_shape=[results] + [jax.ShapeDtypeStruct((hidden, width), jnp.bfloat16)] * 3,
        compiler_params=pltpu.CompilerParams(vmem_limit_bytes=56 * 1024 * 1024),
        cost_estimate=pl.CostEstimate(
            flops=6 * work * hidden, bytes_accessed=4 * work + 6 * hidden * width,
            transcendentals=0,
        ),
    )(jnp.reshape(first, (1,)), *operands)


def on_device(x_saved, routes, gates, cotangent, w_gate, w_up, w_down):
    sections = lax.axis_size("section")
    devices_wide = lax.axis_size("expert")
    section_index = lax.axis_index("section")
    chips = devices_wide // SPLIT
    _, batches, tokens, width = x_saved.shape
    groups = batches // GROUP
    block = GROUP * ROOM
    rows = chips * block
    hidden = w_gate.shape[1]
    same_core = [[SPLIT * c + k for c in range(chips)] for k in range(SPLIT)]
    swap = [(i, i ^ 1) for i in range(devices_wide)]
    ring = [(i, (i - 1) % sections) for i in range(sections)]

    def across(value):
        shaped = value.reshape(chips, -1, width)
        out = lax.all_to_all(shaped, "expert", 0, 0, axis_index_groups=same_core, tiled=True)
        return out.reshape(value.shape)

    def swapped(value):
        return lax.ppermute(value, "expert", swap)

    gate_rows, up_rows, down_rows = w_gate[0], w_up[0], w_down[0]
    both_rows = jnp.concatenate([gate_rows, up_rows], axis=0)

    placing, slot_gates, packing, unpacking = slot_tables(routes[0], gates[0], chips)
    x_tokens = x_saved[0].reshape(batches * tokens, width)
    x_out = dot(packing, x_tokens).astype(jnp.bfloat16)
    x_out, cotangent = together(x_out, cotangent)

    by_group = cotangent.reshape(groups, GROUP * tokens, -1)
    blocks = []
    for ahead in range(sections):
        wanted = (section_index + ahead + 1) % sections
        wanted = jnp.where(wanted < groups, wanted, 0)
        blocks.append(lax.dynamic_index_in_dim(by_group, wanted, 0, keepdims=False))
    x_packed = across(x_out)
    step = 1
    while step < sections:
        moved = [k for k in range(sections) if k & step]
        pairs = [(z, (z + step) % sections) for z in range(sections)]
        sent = jnp.concatenate([blocks[k] for k in moved])
        sent = lax.ppermute(sent, "section", pairs).reshape(len(moved), GROUP * tokens, -1)
        for i, k in enumerate(moved):
            blocks[k] = sent[i]
        step *= 2
    arriving = jnp.concatenate(
        [lax.select_n((section_index - j) % sections, *blocks) for j in range(sections)], axis=1
    )
    padded_placing = jnp.concatenate([placing, jnp.zeros_like(placing[:1])])
    padded_gates = jnp.concatenate([slot_gates, jnp.zeros_like(slot_gates[:1])])
    x_packed, arriving, both_rows, padded_placing, padded_gates, unpacking = together(
        x_packed, arriving, both_rows, padded_placing, padded_gates, unpacking
    )
    x_packed_other = swapped(x_packed)

    def unpacked(packed, count):
        place = unpacking[:count].reshape(count * rows, -1)
        return dot(place, packed).astype(jnp.bfloat16)

    def forward(x):
        pre = dot(x, both_rows, COLS_COLS)
        pre_gate, pre_up = pre[:, :hidden], pre[:, hidden:]
        sigmoid = jax.nn.sigmoid(pre_gate)
        swished = pre_gate * sigmoid
        gate_slope = pre_up * (sigmoid * (1.0 + pre_gate * (1.0 - sigmoid)))
        slope = jnp.concatenate([gate_slope, swished], axis=1)
        return slope, (swished * pre_up).astype(jnp.bfloat16)

    def hidden_part(rows_grad, slope):
        d_hidden = dot(rows_grad, down_rows, COLS_COLS)
        return (jnp.concatenate([d_hidden, d_hidden], axis=1) * slope).astype(jnp.bfloat16)

    def group_at(tick):
        return tick - (sections - 1 - section_index)

    def sliced(value, tick):
        chosen = jnp.clip(group_at(tick), 0, groups - 1)
        return lax.dynamic_slice_in_dim(value, chosen * rows, rows, axis=0)

    kept_out, kept = [], []
    ticks = sections + groups - 1
    for tick in range(ticks):
        group = group_at(tick)
        active = jnp.logical_and(group >= 0, group < groups)
        place = padded_placing[jnp.where(active, group, groups)]
        gate = padded_gates[jnp.where(active, group, groups)]
        if tick == 0:
            rows_out = (dot(place, arriving) * gate[:, None]).astype(jnp.bfloat16)
            rows_out, x_packed = together(rows_out, x_packed)
            came = across(rows_out)
            x_mine = unpacked(x_packed, groups)
            slopes = [forward(x_mine[:rows])[0], forward(unpacked(x_packed_other, 1))[0]]
            rows_mine, slopes, x_mine = together(came, slopes, x_mine)
        elif tick == 1:
            slope_mine = sliced(slope_mine_all, tick)
            arriving, place, gate, slope_mine, x_other = together(
                arriving, place, gate, slope_mine, x_other
            )
            rows_out = (dot(place, arriving) * gate[:, None]).astype(jnp.bfloat16)
            rows_out, x_other = together(rows_out, x_other)
            came = across(rows_out)
            slope_other_all, act_other = forward(x_other)
            rows_mine, slope_other = together(came, sliced(slope_other_all, tick))
            slopes = [slope_mine, slope_other]
            x_halves, act_halves = [
                [value.reshape(groups, rows, -1) for value in values]
                for values in ((x_mine, x_other), (act_mine, act_other))
            ]
        else:
            slopes = [sliced(slope_mine_all, tick), sliced(slope_other_all, tick)]
            arriving, place, gate, slopes = together(arriving, place, gate, slopes)
            rows_mine = across((dot(place, arriving) * gate[:, None]).astype(jnp.bfloat16))
        rows_other = swapped(rows_mine)
        d_mine = hidden_part(rows_mine, slopes[0])
        d_mine, rows_other = together(d_mine, rows_other)
        d_other = hidden_part(rows_other, slopes[1])
        part_other = dot(d_other, both_rows).astype(jnp.bfloat16)
        from_other = swapped(part_other)
        part_mine = dot(d_mine, both_rows).astype(jnp.bfloat16)
        part_mine, from_other = together(part_mine, from_other)
        summed = part_mine.astype(jnp.float32) + from_other.astype(jnp.float32)
        summed = summed.astype(jnp.bfloat16)
        if tick == 0:
            summed, x_mine = together(summed, x_mine)
            slope_mine_all, act_mine = forward(x_mine)
        if tick == ticks - 1:
            first = sections - 1 - section_index
            summed, d_mine, d_other, rows_mine, rows_other, first = together(
                summed, d_mine, d_other, rows_mine, rows_other, first
            )
        kept.append((d_mine, d_other, rows_mine, rows_other))
        returned = across(summed)
        if tick == ticks - 1:
            results, *grads = weight_grads(
                first, kept, kept_out, x_halves, act_halves, sections, batches
            )
            returned, results, grads = together(returned, results, grads)
        outgoing = (arriving.astype(jnp.float32) + dot(place, returned, ROWS_ROWS)).astype(
            jnp.bfloat16
        )
        if tick == 0:
            outgoing, x_packed_other = together(outgoing, x_packed_other)
            x_other = unpacked(x_packed_other, groups)
        if tick < ticks - 1:
            kept_out.append(outgoing)
            arriving = lax.ppermute(outgoing, "section", ring)

    last = results[-GROUP * tokens :]
    last = jnp.where(section_index == 0, outgoing, last)
    results = lax.dynamic_update_slice(results, last, (results.shape[0] - GROUP * tokens, 0))
    return (results.reshape(1, batches, tokens, width),) + tuple(g[None] for g in grads)


def solution(mesh):
    in_specs = (
        P("section", None, "expert", None),
        P("section", None, "expert", None),
        P("section", None, "expert", None),
        P(None, "expert", "section"),
        P("section", "expert", None),
        P("section", "expert", None),
        P("section", "expert", None),
    )
    out_specs = (
        P("section", None, "expert", None),
        P("section", "expert", None),
        P("section", "expert", None),
        P("section", "expert", None),
    )
    return jax.shard_map(
        on_device, mesh=mesh, in_specs=in_specs, out_specs=out_specs, check_vma=False
    )
```

```python
from functools import partial

import jax
import jax.numpy as jnp
from jax import lax
from jax.experimental import pallas as pl
from jax.experimental.pallas import tpu as pltpu
from jax.sharding import PartitionSpec as P

SPLIT = 2
GROUP = 2
ROOM = 4
CAP = 3
CHUNKS = 2

ROWS_ROWS = (((0,), (0,)), ((), ()))
COLS_COLS = (((1,), (1,)), ((), ()))


def dot(left, right, dims=(((1,), (0,)), ((), ()))):
    return lax.dot_general(left, right, dims, preferred_element_type=jnp.float32)


def together(*values):
    return lax.optimization_barrier(values)


def slot_tables(routes, gates, experts):
    batches, tokens, top = routes.shape
    groups = batches // GROUP
    rows = tokens * top
    flat = routes.reshape(batches, rows)
    same = flat[:, :, None] == flat[:, None, :]
    before = jnp.arange(rows)[:, None] > jnp.arange(rows)[None, :]
    position = jnp.sum(jnp.logical_and(same, before[None]).astype(jnp.int32), axis=2)
    batch = jnp.arange(batches, dtype=jnp.int32)[:, None]
    slot = flat * (GROUP * ROOM) + batch % GROUP * ROOM + position
    slot = slot.reshape(groups, 1, GROUP * tokens, top)
    slots = jnp.arange(experts * GROUP * ROOM, dtype=jnp.int32)
    hit = slots[None, :, None, None] == slot
    gate = jnp.where(hit, gates.reshape(groups, 1, GROUP * tokens, top), 0.0)
    placing = jnp.any(hit, axis=3).astype(jnp.bfloat16)
    pack = (flat * batches + batch) * CAP + position
    packs = jnp.arange(experts * batches * CAP, dtype=jnp.int32)
    packing = packs[:, None, None] == pack.reshape(1, batches * tokens, top)
    packing = jnp.any(packing, axis=2).astype(jnp.bfloat16)
    half, place = slots % (GROUP * ROOM) // ROOM, slots % ROOM
    source = slots // (GROUP * ROOM) * batches + half
    source = source + jnp.arange(groups, dtype=jnp.int32)[:, None] * GROUP
    source = jnp.where(place < CAP, source * CAP + place, -1)
    unpacking = (source[:, :, None] == packs[None, None, :]).astype(jnp.bfloat16)
    return placing, jnp.sum(gate, axis=(2, 3)), packing, unpacking


def grads_kernel(sections, batches, first_ref, *refs):
    groups = refs[-5].shape[0]
    ticks = sections + groups - 1
    kept = [refs[4 * t : 4 * t + 4] for t in range(ticks)]
    x_halves, act_halves = refs[4 * ticks : 4 * ticks + 2], refs[4 * ticks + 2 : 4 * ticks + 4]
    kept_out, results = refs[4 * ticks + 4 : 5 * ticks + 3], refs[5 * ticks + 3]
    outs = refs[5 * ticks + 4 : 5 * ticks + 7]
    d_buf, act_buf, rows_buf, x_buf, sems = refs[-5:]
    chunk = rows_buf.shape[-1]
    hidden = act_buf.shape[-1]
    step = pl.program_id(0)
    pairs = [(g, h) for g in range(groups) for h in range(SPLIT)]

    def columns(c):
        return pl.ds(c * chunk, chunk)

    def d_copies(first):
        return [
            pltpu.make_async_copy(kept[first + g][h], d_buf.at[g, h], sems.at[g * SPLIT + h])
            for g, h in pairs
        ]

    def act_copies():
        at = len(pairs)
        return [
            pltpu.make_async_copy(act_halves[h], act_buf.at[:, h], sems.at[at + h])
            for h in range(SPLIT)
        ]

    def x_copies(c):
        at = len(pairs) + SPLIT + c * SPLIT
        return [
            pltpu.make_async_copy(
                x_halves[h].at[:, :, columns(c)], x_buf.at[c, :, h], sems.at[at + h]
            )
            for h in range(SPLIT)
        ]

    def row_copies(c, first):
        at = len(pairs) + SPLIT + CHUNKS * SPLIT + c * len(pairs)
        return [
            pltpu.make_async_copy(
                kept[first + g][SPLIT + h].at[:, columns(c)],
                rows_buf.at[c, g, h],
                sems.at[at + g * SPLIT + h],
            )
            for g, h in pairs
        ]

    def result_copies(first):
        at = len(pairs) + SPLIT + CHUNKS * (SPLIT + len(pairs))
        block = kept_out[0].shape[0]
        return [
            pltpu.make_async_copy(
                kept_out[min(first + g, ticks - 2)],
                results.at[pl.ds(g * block, block)],
                sems.at[at + g],
            )
            for g in range(groups)
        ]

    @pl.when(step == 0)
    def start():
        for first in range(sections):

            @pl.when(first_ref[0] == first)
            def start_kept():
                copies = d_copies(first) + x_copies(0) + act_copies() + row_copies(0, first)
                for c in range(1, CHUNKS):
                    copies = copies + x_copies(c) + row_copies(c, first)
                for copy in copies + result_copies(first):
                    copy.start()

        for copy in d_copies(0):
            copy.wait()

    def merged(value):
        return value.reshape(-1, value.shape[-1])

    for c in range(CHUNKS):

        @pl.when(step == c)
        def compute():
            for copy in x_copies(c):
                copy.wait()
            both = dot(merged(d_buf[...]), merged(x_buf[c]), ROWS_ROWS) / batches
            outs[0][...] = both[:hidden].astype(jnp.bfloat16)
            outs[1][...] = both[hidden:].astype(jnp.bfloat16)
            for copy in row_copies(c, 0) + (act_copies() if c == 0 else []):
                copy.wait()
            down = dot(merged(act_buf[...]), merged(rows_buf[c]), ROWS_ROWS) / batches
            outs[2][...] = down.astype(jnp.bfloat16)
            if c == CHUNKS - 1:
                for copy in result_copies(0):
                    copy.wait()


def weight_grads(first, kept, kept_out, x_halves, act_halves, sections, batches):
    groups, rows, width = x_halves[0].shape
    hidden = act_halves[0].shape[2]
    chunk = width // CHUNKS
    operands = [value for tick in kept for value in tick] + list(x_halves) + list(act_halves)
    operands = operands + kept_out
    anywhere = pl.BlockSpec(memory_space=pl.ANY)
    copies = (1 + CHUNKS) * (groups + 1) * SPLIT + groups
    results = jax.ShapeDtypeStruct((groups * kept_out[0].shape[0], width), jnp.bfloat16)
    halves = (groups, SPLIT, rows)
    work = groups * SPLIT * rows * width
    return pl.pallas_call(
        partial(grads_kernel, sections, batches),
        grid_spec=pltpu.PrefetchScalarGridSpec(
            num_scalar_prefetch=1,
            grid=(CHUNKS,),
            in_specs=[anywhere] * len(operands),
            out_specs=[pl.BlockSpec(results.shape, lambda n, first: (0, 0))]
            + [pl.BlockSpec((hidden, chunk), lambda n, first: (0, n))] * 3,
            scratch_shapes=[
                pltpu.VMEM(halves + (2 * hidden,), jnp.bfloat16),
                pltpu.VMEM(halves + (hidden,), jnp.bfloat16),
                pltpu.VMEM((CHUNKS,) + halves + (chunk,), jnp.bfloat16),
                pltpu.VMEM((CHUNKS,) + halves + (chunk,), jnp.bfloat16),
                pltpu.SemaphoreType.DMA((copies,)),
            ],
        ),
        out_shape=[results] + [jax.ShapeDtypeStruct((hidden, width), jnp.bfloat16)] * 3,
        compiler_params=pltpu.CompilerParams(vmem_limit_bytes=56 * 1024 * 1024),
        cost_estimate=pl.CostEstimate(
            flops=6 * work * hidden, bytes_accessed=4 * work + 6 * hidden * width,
            transcendentals=0,
        ),
    )(jnp.reshape(first, (1,)), *operands)


def on_device(x_saved, routes, gates, cotangent, w_gate, w_up, w_down):
    sections = lax.axis_size("section")
    devices_wide = lax.axis_size("expert")
    section_index = lax.axis_index("section")
    chips = devices_wide // SPLIT
    _, batches, tokens, width = x_saved.shape
    groups = batches // GROUP
    block = GROUP * ROOM
    rows = chips * block
    hidden = w_gate.shape[1]
    same_core = [[SPLIT * c + k for c in range(chips)] for k in range(SPLIT)]
    swap = [(i, i ^ 1) for i in range(devices_wide)]
    ring = [(i, (i - 1) % sections) for i in range(sections)]

    def across(value):
        shaped = value.reshape(chips, -1, width)
        out = lax.all_to_all(shaped, "expert", 0, 0, axis_index_groups=same_core, tiled=True)
        return out.reshape(value.shape)

    def swapped(value):
        return lax.ppermute(value, "expert", swap)

    gate_rows, up_rows, down_rows = w_gate[0], w_up[0], w_down[0]
    both_rows = jnp.concatenate([gate_rows, up_rows], axis=0)

    placing, slot_gates, packing, unpacking = slot_tables(routes[0], gates[0], chips)
    x_tokens = x_saved[0].reshape(batches * tokens, width)
    x_out = dot(packing, x_tokens).astype(jnp.bfloat16)
    x_out, cotangent = together(x_out, cotangent)

    by_group = cotangent.reshape(groups, GROUP * tokens, -1)
    blocks = []
    for ahead in range(sections):
        wanted = (section_index + ahead + 1) % sections
        wanted = jnp.where(wanted < groups, wanted, 0)
        blocks.append(lax.dynamic_index_in_dim(by_group, wanted, 0, keepdims=False))
    x_packed = across(x_out)
    step = 1
    while step < sections:
        moved = [k for k in range(sections) if k & step]
        pairs = [(z, (z + step) % sections) for z in range(sections)]
        sent = jnp.concatenate([blocks[k] for k in moved])
        sent = lax.ppermute(sent, "section", pairs).reshape(len(moved), GROUP * tokens, -1)
        for i, k in enumerate(moved):
            blocks[k] = sent[i]
        step *= 2
    arriving = jnp.concatenate(
        [lax.select_n((section_index - j) % sections, *blocks) for j in range(sections)], axis=1
    )
    padded_placing = jnp.concatenate([placing, jnp.zeros_like(placing[:1])])
    padded_gates = jnp.concatenate([slot_gates, jnp.zeros_like(slot_gates[:1])])
    x_packed, arriving, both_rows, padded_placing, padded_gates, unpacking = together(
        x_packed, arriving, both_rows, padded_placing, padded_gates, unpacking
    )
    x_packed_other = swapped(x_packed)

    def unpacked(packed, count):
        place = unpacking[:count].reshape(count * rows, -1)
        return dot(place, packed).astype(jnp.bfloat16)

    def forward(x):
        pre = dot(x, both_rows, COLS_COLS)
        pre_gate, pre_up = pre[:, :hidden], pre[:, hidden:]
        sigmoid = jax.nn.sigmoid(pre_gate)
        swished = pre_gate * sigmoid
        gate_slope = pre_up * (sigmoid * (1.0 + pre_gate * (1.0 - sigmoid)))
        slope = jnp.concatenate([gate_slope, swished], axis=1)
        return slope, (swished * pre_up).astype(jnp.bfloat16)

    def hidden_part(rows_grad, slope):
        d_hidden = dot(rows_grad, down_rows, COLS_COLS)
        return (jnp.concatenate([d_hidden, d_hidden], axis=1) * slope).astype(jnp.bfloat16)

    def group_at(tick):
        return tick - (sections - 1 - section_index)

    def sliced(value, tick):
        chosen = jnp.clip(group_at(tick), 0, groups - 1)
        return lax.dynamic_slice_in_dim(value, chosen * rows, rows, axis=0)

    kept_out, kept = [], []
    ticks = sections + groups - 1
    for tick in range(ticks):
        group = group_at(tick)
        active = jnp.logical_and(group >= 0, group < groups)
        place = padded_placing[jnp.where(active, group, groups)]
        gate = padded_gates[jnp.where(active, group, groups)]
        if tick == 0:
            rows_out = (dot(place, arriving) * gate[:, None]).astype(jnp.bfloat16)
            rows_out, x_packed = together(rows_out, x_packed)
            came = across(rows_out)
            x_mine = unpacked(x_packed, groups)
            (x_first,) = together(unpacked(x_packed_other, 1))
            slopes = [forward(x_mine[:rows])[0], forward(x_first)[0]]
            rows_mine, slopes, x_mine = together(came, slopes, x_mine)
        elif tick == 1:
            slope_mine = sliced(slope_mine_all, tick)
            arriving, place, gate, slope_mine, x_other = together(
                arriving, place, gate, slope_mine, x_other
            )
            rows_out = (dot(place, arriving) * gate[:, None]).astype(jnp.bfloat16)
            rows_out, x_other = together(rows_out, x_other)
            came = across(rows_out)
            slope_other_all, act_other = forward(x_other)
            rows_mine, slope_other = together(came, sliced(slope_other_all, tick))
            slopes = [slope_mine, slope_other]
            x_halves, act_halves = [
                [value.reshape(groups, rows, -1) for value in values]
                for values in ((x_mine, x_other), (act_mine, act_other))
            ]
        else:
            slopes = [sliced(slope_mine_all, tick), sliced(slope_other_all, tick)]
            arriving, place, gate, slopes = together(arriving, place, gate, slopes)
            rows_mine = across((dot(place, arriving) * gate[:, None]).astype(jnp.bfloat16))
        rows_other = swapped(rows_mine)
        d_mine = hidden_part(rows_mine, slopes[0])
        d_mine, rows_other = together(d_mine, rows_other)
        d_other = hidden_part(rows_other, slopes[1])
        part_other = dot(d_other, both_rows).astype(jnp.bfloat16)
        from_other = swapped(part_other)
        part_mine = dot(d_mine, both_rows).astype(jnp.bfloat16)
        part_mine, from_other = together(part_mine, from_other)
        summed = part_mine.astype(jnp.float32) + from_other.astype(jnp.float32)
        summed = summed.astype(jnp.bfloat16)
        if tick == 0:
            summed, x_mine = together(summed, x_mine)
            slope_mine_all, act_mine = forward(x_mine)
        if tick == ticks - 1:
            first = sections - 1 - section_index
            summed, d_mine, d_other, rows_mine, rows_other, first = together(
                summed, d_mine, d_other, rows_mine, rows_other, first
            )
        kept.append((d_mine, d_other, rows_mine, rows_other))
        returned = across(summed)
        if tick == ticks - 1:
            results, *grads = weight_grads(
                first, kept, kept_out, x_halves, act_halves, sections, batches
            )
            returned, results, grads = together(returned, results, grads)
        outgoing = (arriving.astype(jnp.float32) + dot(place, returned, ROWS_ROWS)).astype(
            jnp.bfloat16
        )
        if tick == 0:
            outgoing, x_packed_other = together(outgoing, x_packed_other)
            x_other = unpacked(x_packed_other, groups)
        if tick < ticks - 1:
            kept_out.append(outgoing)
            arriving = lax.ppermute(outgoing, "section", ring)

    last = results[-GROUP * tokens :]
    last = jnp.where(section_index == 0, outgoing, last)
    results = lax.dynamic_update_slice(results, last, (results.shape[0] - GROUP * tokens, 0))
    return (results.reshape(1, batches, tokens, width),) + tuple(g[None] for g in grads)


def solution(mesh):
    in_specs = (
        P("section", None, "expert", None),
        P("section", None, "expert", None),
        P("section", None, "expert", None),
        P(None, "expert", "section"),
        P("section", "expert", None),
        P("section", "expert", None),
        P("section", "expert", None),
    )
    out_specs = (
        P("section", None, "expert", None),
        P("section", "expert", None),
        P("section", "expert", None),
        P("section", "expert", None),
    )
    return jax.shard_map(
        on_device, mesh=mesh, in_specs=in_specs, out_specs=out_specs, check_vma=False
    )
```
